32 devices in a mesh: leaf: 32 (over z, y, x, core).
Axes of the slice: x: 2, y: 2, z: 4, core: 2. Of those that a mesh axis runs over, the one named last changes fastest.
Arguments:
- vectors: float32 [32, 512, 128], P('leaf'), may hold values from -6 to 6
- points: float32 [32, 3, 512], P('leaf')
- leaf_basis: float32 [32, 512, 128], P('leaf'), may hold values from -0.25 to 0.25
- transfer_leaf: float32 [32, 128, 128], P('leaf'), may hold values from -0.5 to 0.5
- transfer_pair: float32 [2048, 128], P('leaf'), may hold values from -0.5 to 0.5
- transfer_quad: float32 [1024, 128], P('leaf'), may hold values from -0.5 to 0.5
- skel_leaf: float32 [32, 3, 128], P('leaf')
- skel_pair: float32 [16, 3, 128], replicated
- skel_quad: float32 [8, 3, 128], replicated
- skel_top: float32 [4, 3, 128], replicated
- near_list: int32 [32, 16], P('leaf'), may hold values from -1 to 31, as said below
- far_leaf: int32 [32, 8], P('leaf'), may hold values from -1 to 31, as said below
- far_pair: int32 [16, 8], replicated, may hold values from -1 to 15, as said below
- far_quad: int32 [8, 8], replicated, may hold values from -1 to 7, as said below
- far_top: int32 [4, 8], replicated, may hold values from -1 to 3, as said below
Outputs:
- product: float32 [32, 512, 128], P('leaf')
The draws below stay inside these ranges and needn't reach their ends.
Inputs may be any that keep to these rules, and one draw needn't show every extreme that they name: `near_list`: entry 0 of row l is l; the other entries are distinct leaves within 8 of l, or -1 for an unused slot. `far_leaf`: distinct leaves within 8 of the row's leaf, none of them in that leaf's row of near_list, or -1 for an unused slot. `far_pair`: distinct clusters within 4 of the row's cluster and other than it, or -1 for an unused slot. `far_quad`: distinct clusters within 4 of the row's cluster and other than it, or -1 for an unused slot. `far_top`: distinct top clusters other than the row's cluster, or -1 for an unused slot.
All inputs are finite; a program needn't handle non-finite values.
Results may differ from the reference program's by a relative error of at most 0.0003.
Values sent between devices are 32-bit elements; how exact they have to be, the bound alone decides.
No kernel may reach another device: no remote copies, remote signals or barrier semaphores. Data moves between devices by JAX's collectives and lax.ppermute only.
A program may use at most 64 MiB of HBM per device.

```python
import jax
import jax.numpy as jnp
from jax import lax

LEAF = 512
RANK = 128
NVEC = 128
NEAR = 16
FAR = 8
REACH = 8
FAR_REACH = 4
LEAVES = 32


def corner_of(leaf_ids):
    first = jnp.zeros(leaf_ids.shape, jnp.float32)
    second = jnp.zeros(leaf_ids.shape, jnp.float32)
    third = jnp.zeros(leaf_ids.shape, jnp.float32)
    for bit_index in range(15):
        digit = (leaf_ids // 2 ** bit_index % 2).astype(jnp.float32) * float(2 ** (bit_index // 3))
        if bit_index % 3 == 0:
            first = first + digit
        elif bit_index % 3 == 1:
            second = second + digit
        else:
            third = third + digit
    return jnp.stack([first, second, third], axis=-2)


def draw_points(key, part):
    corners = corner_of(jnp.arange(LEAVES)[:, None])
    return corners + jax.random.uniform(key, (LEAVES, 3, LEAF), jnp.float32)


def skeleton_draw(key, level):
    clusters = LEAVES // 2 ** level
    first_key, second_key = jax.random.split(jax.random.fold_in(key, 31 + level))
    common = 8.0 * jax.random.uniform(first_key, (1, 3, RANK), jnp.float32)
    jitter = 0.15 * jax.random.uniform(second_key, (clusters, 3, RANK), jnp.float32)
    return common + jitter


def draw_skel_leaf(key, part):
    return skeleton_draw(key, 0)


def draw_skel_pair(key, part):
    return skeleton_draw(key, 1)


def draw_skel_quad(key, part):
    return skeleton_draw(key, 2)


def draw_skel_top(key, part):
    return skeleton_draw(key, 3)


def shuffled_offsets(key, rows, reach):
    offsets = jnp.concatenate([jnp.arange(-reach, 0), jnp.arange(1, reach + 1)]).astype(jnp.int32)
    scores = jax.random.randint(key, (rows, 2 * reach), 0, 1 << 20) * (2 * reach) + jnp.arange(2 * reach)[None, :]
    return offsets[jnp.argsort(scores, axis=1)]


def leaf_lists(key):
    first_key, second_key = jax.random.split(jax.random.fold_in(key, 11))
    chosen = shuffled_offsets(first_key, LEAVES, REACH)
    leaf_ids = jnp.arange(LEAVES).astype(jnp.int32)
    near_count = jax.random.randint(second_key, (LEAVES,), 1, NEAR + 1)
    near_count = jnp.where(leaf_ids % 5 == 0, NEAR, jnp.where(leaf_ids % 5 == 1, 1, near_count))
    targets = leaf_ids[:, None] + chosen
    inside = (targets >= 0) & (targets < LEAVES)
    slot_ids = jnp.arange(2 * REACH)[None, :]
    near_rest = jnp.where((slot_ids < near_count[:, None] - 1) & inside, targets, -1)[:, :NEAR - 1]
    near_rows = jnp.concatenate([leaf_ids[:, None], near_rest], axis=1)
    source = near_count[:, None] - 1 + jnp.arange(FAR)[None, :]
    bounded = jnp.minimum(source, 2 * REACH - 1)
    picked = jnp.take_along_axis(targets, bounded, axis=1)
    picked_inside = jnp.take_along_axis(inside, bounded, axis=1)
    far_rows = jnp.where((source < 2 * REACH) & picked_inside, picked, -1)
    return (near_rows.astype(jnp.int32), far_rows.astype(jnp.int32))


def draw_near_list(key, part):
    return leaf_lists(key)[0]


def draw_far_leaf(key, part):
    return leaf_lists(key)[1]


def cluster_lists(key, level):
    clusters = LEAVES // 2 ** level
    first_key, second_key = jax.random.split(jax.random.fold_in(key, 51 + level))
    chosen = shuffled_offsets(first_key, clusters, FAR_REACH)[:, :FAR]
    cluster_ids = jnp.arange(clusters).astype(jnp.int32)
    counts = jax.random.randint(second_key, (clusters,), 1, FAR + 1)
    counts = jnp.where(cluster_ids % 5 == 0, FAR, counts)
    targets = cluster_ids[:, None] + chosen
    inside = (targets >= 0) & (targets < clusters)
    slot_ids = jnp.arange(FAR)[None, :]
    return jnp.where((slot_ids < counts[:, None]) & inside, targets, -1).astype(jnp.int32)


def draw_far_pair(key, part):
    return cluster_lists(key, 1)


def draw_far_quad(key, part):
    return cluster_lists(key, 2)


def draw_far_top(key, part):
    clusters = LEAVES // 8
    most = min(FAR, clusters - 1)
    first_key, second_key = jax.random.split(jax.random.fold_in(key, 77))
    offsets = jnp.arange(1, clusters).astype(jnp.int32)
    scores = jax.random.randint(first_key, (clusters, clusters - 1), 0, 1 << 20) * clusters + jnp.arange(clusters - 1)[None, :]
    chosen = offsets[jnp.argsort(scores, axis=1)][:, :most]
    cluster_ids = jnp.arange(clusters).astype(jnp.int32)
    counts = jax.random.randint(second_key, (clusters,), 1, most + 1)
    counts = jnp.where(cluster_ids % 5 == 0, most, counts)
    slot_ids = jnp.arange(most)[None, :]
    entries = jnp.where(slot_ids < counts[:, None], (cluster_ids[:, None] + chosen) % clusters, -1)
    padding = jnp.full((clusters, FAR - most), -1, jnp.int32)
    return jnp.concatenate([entries.astype(jnp.int32), padding], axis=1)


def level_of(rng, shape, shards, smallest, largest):
    def one(axis_at, shards_of):
        draws = jax.random.uniform(jax.random.fold_in(jax.random.fold_in(rng, 6), axis_at), (shards_of,), jnp.float32, smallest / len(shards), largest / len(shards))
        return jnp.repeat(jnp.exp(draws), shape[axis_at] // shards_of).reshape((-1,) + (1,) * (len(shape) - axis_at - 1))

    loudness = one(*shards[0])
    for cut in shards[1:]:
        loudness = loudness * one(*cut)
    return loudness


def gaussian(rng, dims, scale, bound, shards=(), kind=jnp.bfloat16):
    values = scale * jax.random.normal(rng, dims, jnp.float32)
    if shards:
        values = values * level_of(rng, dims, shards, -0.22, 0.18)
    return jnp.clip(values, -bound, bound).astype(kind)


def setup_inputs(seed: int = 0) -> dict:
    arg_keys = jax.random.split(jax.random.key(seed), 16)
    return {
        "vectors": gaussian(arg_keys[0], (LEAVES, LEAF, NVEC), 1.0, 6.0, ((0, 32),), jnp.float32),
        "points": draw_points(jax.random.fold_in(arg_keys[15], 71), 0),
        "leaf_basis": gaussian(arg_keys[2], (LEAVES, LEAF, RANK), LEAF ** -0.5, 0.25, ((0, 32),), jnp.float32),
        "transfer_leaf": gaussian(arg_keys[3], (LEAVES, RANK, RANK), RANK ** -0.5, 0.5, ((0, 32),), jnp.float32),
        "transfer_pair": gaussian(arg_keys[4], (LEAVES // 2 * RANK, RANK), RANK ** -0.5, 0.5, ((0, 32),), jnp.float32),
        "transfer_quad": gaussian(arg_keys[5], (LEAVES // 4 * RANK, RANK), RANK ** -0.5, 0.5, ((0, 32),), jnp.float32),
        "skel_leaf": draw_skel_leaf(jax.random.fold_in(arg_keys[15], 71), 0),
        "skel_pair": draw_skel_pair(jax.random.fold_in(arg_keys[15], 71), 0),
        "skel_quad": draw_skel_quad(jax.random.fold_in(arg_keys[15], 71), 0),
        "skel_top": draw_skel_top(jax.random.fold_in(arg_keys[15], 71), 0),
        "near_list": draw_near_list(jax.random.fold_in(arg_keys[15], 71), 0),
        "far_leaf": draw_far_leaf(jax.random.fold_in(arg_keys[15], 71), 0),
        "far_pair": draw_far_pair(jax.random.fold_in(arg_keys[15], 71), 0),
        "far_quad": draw_far_quad(jax.random.fold_in(arg_keys[15], 71), 0),
        "far_top": draw_far_top(jax.random.fold_in(arg_keys[15], 71), 0),
    }


INV_FOUR_PI = 0.07957747154594767
DELTA_SQ = 0.01
HIGHEST = lax.Precision.HIGHEST

def kernel_block(left_pts, right_pts):
    distance = jnp.zeros((left_pts.shape[1], right_pts.shape[1]), jnp.float32)
    for axis_id in range(3):
        offset_gap = left_pts[axis_id][:, None] - right_pts[axis_id][None, :]
        distance = distance + offset_gap * offset_gap
    return INV_FOUR_PI * lax.rsqrt(distance + DELTA_SQ)

def listed_sum(own_coords, entries, coords_all, values_all, width):

    def advance(running, partner):
        chosen = jnp.maximum(partner, 0)
        contrib = jnp.dot(kernel_block(own_coords, coords_all[chosen]), values_all[chosen], precision=HIGHEST)
        return (running + jnp.where(partner >= 0, contrib, 0.0), None)
    start_value = jnp.zeros((own_coords.shape[1], width), jnp.float32)
    result, _ = lax.scan(advance, start_value, entries)
    return result

def far_level(skeletons, lists, coefs):
    width = coefs.shape[2]

    def single(cluster):
        return listed_sum(skeletons[cluster], lists[cluster], skeletons, coefs, width)
    return lax.map(single, jnp.arange(skeletons.shape[0]))

def reference(vectors, points, leaf_basis, transfer_leaf, transfer_pair, transfer_quad, skel_leaf, skel_pair, skel_quad, skel_top, near_list, far_leaf, far_pair, far_quad, far_top):
    width = vectors.shape[2]

    def near_single(leaf_id):
        return listed_sum(points[leaf_id], near_list[leaf_id], points, vectors, width)
    near_field = lax.map(near_single, jnp.arange(vectors.shape[0]))
    pair_mats = transfer_pair.reshape(-1, RANK, RANK)
    quad_mats = transfer_quad.reshape(-1, RANK, RANK)
    coef_leaf = jnp.einsum('lpr,lpv->lrv', leaf_basis, vectors, precision=HIGHEST)
    coef_pair = jnp.einsum('lrs,lrv->lsv', transfer_leaf, coef_leaf, precision=HIGHEST).reshape(-1, 2, RANK, width).sum(axis=1)
    coef_quad = jnp.einsum('crs,crv->csv', pair_mats, coef_pair, precision=HIGHEST).reshape(-1, 2, RANK, width).sum(axis=1)
    coef_top = jnp.einsum('crs,crv->csv', quad_mats, coef_quad, precision=HIGHEST).reshape(-1, 2, RANK, width).sum(axis=1)
    local_top = far_level(skel_top, far_top, coef_top)
    local_quad = far_level(skel_quad, far_quad, coef_quad) + jnp.einsum('crs,csv->crv', quad_mats, jnp.repeat(local_top, 2, axis=0), precision=HIGHEST)
    local_pair = far_level(skel_pair, far_pair, coef_pair) + jnp.einsum('crs,csv->crv', pair_mats, jnp.repeat(local_quad, 2, axis=0), precision=HIGHEST)
    local_leaf = far_level(skel_leaf, far_leaf, coef_leaf) + jnp.einsum('crs,csv->crv', transfer_leaf, jnp.repeat(local_pair, 2, axis=0), precision=HIGHEST)
    return near_field + jnp.einsum('lpr,lrv->lpv', leaf_basis, local_leaf, precision=HIGHEST)
```

```python
import functools

import jax
import jax.numpy as jnp
from jax import lax
from jax.experimental import pallas as pl
from jax.experimental.pallas import tpu as pltpu
from jax.sharding import PartitionSpec as P

INV_FOUR_PI = 0.07957747154594767
DELTA_SQ = 0.01
HIGHEST = lax.Precision.HIGHEST
AXIS = "leaf"

PLANE = 8
NEAR_SLOTS = 16
FAR_SLOTS = 8

VEC = 0
META = 512
COEF = 528
CPAIR = 656
EPAIR = 720
EQUAD = 784
SHIP = 816

VMEM = pl.BlockSpec(memory_space=pltpu.VMEM)
SMEM = pl.BlockSpec(memory_space=pltpu.SMEM)


def call(body, outs, ins, n_smem=0, scratch=(), flops=0, nbytes=0):
    return pl.pallas_call(
        body,
        out_shape=outs,
        in_specs=[SMEM] * n_smem + [VMEM] * (len(ins) - n_smem),
        out_specs=jax.tree.map(lambda _: VMEM, outs),
        scratch_shapes=list(scratch),
        compiler_params=pltpu.CompilerParams(vmem_limit_bytes=32 * 1024 * 1024),
        cost_estimate=pl.CostEstimate(flops=flops, bytes_accessed=nbytes, transcendentals=0),
    )(*ins)


def f32(*shape):
    return jax.ShapeDtypeStruct(shape, jnp.float32)


def dot(a, b):
    return jnp.dot(a, b, precision=HIGHEST, preferred_element_type=jnp.float32)


def dot_t(a, b):
    return lax.dot_general(
        a, b, (((0,), (0,)), ((), ())), precision=HIGHEST, preferred_element_type=jnp.float32
    )


def columns(rows):
    pad = jnp.zeros((128 - rows.shape[0], 128), jnp.float32)
    return jnp.concatenate([rows, pad], axis=0).T


def green(cols, rows):
    dx = cols[0] - rows[0]
    dy = cols[1] - rows[1]
    dz = cols[2] - rows[2]
    return lax.rsqrt((dx * dx + dy * dy) + dz * dz + DELTA_SQ)


def green_of(cols, skel):
    return green([cols[:, a : a + 1] for a in range(3)], [skel[a : a + 1, :] for a in range(3)])


def window_bits(list_ref, row, start, count, base):
    bits = jnp.int32(0)
    for e in range(count):
        entry = list_ref[row, start + e]
        shift = jnp.clip(entry - base, 0, 31)
        bits = bits | jnp.where(entry >= 0, jnp.left_shift(jnp.int32(1), shift), 0)
    return bits


def has(bits, place):
    return (jnp.right_shift(bits, jnp.clip(place, 0, 31)) & 1) == 1


def chips_of(device):
    chip = device // 2
    place = chip % 4
    odd = (chip // 4) % 2
    out = [chip, chip ^ 1, chip ^ 2, chip ^ 3, chip ^ 4, chip + jnp.where(odd == 1, 4, -4)]
    for m in (1, 2, 3):
        other = place ^ m
        out.append((chip ^ m) + jnp.where(place < other, -4, 4))
    return out


def prepare_kernel(idx, vec, pts, skel, basis, move, epair, equad, ship, keep, send):
    core = idx[0] % 2
    ship[VEC : VEC + 512, :] = vec[0]
    zero = jnp.zeros((1, 128), jnp.float32)
    pieces = []
    for k in range(4):
        for a in range(3):
            pieces.append(pts[0, a : a + 1, 128 * k : 128 * (k + 1)])
        pieces.append(skel[0, k : k + 1, :] if k < 3 else zero)
    meta = jnp.concatenate(pieces, axis=0)
    ship[META : META + 16, :] = meta
    coef = dot_t(basis[0], vec[0])
    ship[COEF : COEF + 128, :] = coef
    up = dot_t(move[0], coef)
    ship[CPAIR : CPAIR + 64, :] = jnp.zeros((64, 128), jnp.float32)
    ship[EPAIR : EPAIR + 64, :] = epair[...]
    ship[EQUAD : EQUAD + 32, :] = equad[...]
    low, high = up[:64], up[64:]
    keep[...] = jnp.where(core == 0, low, high)
    send[0:64, :] = jnp.where(core == 0, high, low)
    send[64:80, :] = meta


def near_kernel(slots, first, idx, own_list, sib_list, meta_own, meta_sib, *refs):
    n = len(slots)
    blocks = refs[:n]
    refs = refs[n:]
    if not first:
        total_in, refs = refs[0], refs[1:]
    total, values, cols, high, low = refs
    device = idx[0]
    core = device % 2
    if first:
        total[...] = jnp.zeros_like(total)
    else:
        total[...] = total_in[...]
    chips = chips_of(device)
    bits = []
    for s, (listed, leaf) in enumerate(((own_list, device), (sib_list, device ^ 1))):
        bits.append(window_bits(listed, 0, 0, NEAR_SLOTS, leaf - 9))
    cols[0:128, :] = columns(meta_own[...])
    cols[128:256, :] = columns(meta_sib[...])
    for b, slot in enumerate(slots):
        leaf = 2 * chips[slot] + core
        block = blocks[b]
        v = block[VEC : VEC + 512, :] * INV_FOUR_PI
        vh = v.astype(jnp.bfloat16)
        values[:, 0:128] = vh
        values[:, 128:256] = (v - vh.astype(jnp.float32)).astype(jnp.bfloat16)
        for s in range(2):

            @pl.when(has(bits[s], leaf - ((device ^ s) - 9)))
            def _(block=block, s=s):
                for i in range(4):
                    col = [
                        jnp.broadcast_to(cols[128 * s : 128 * (s + 1), 4 * i + a : 4 * i + a + 1], (128, 128))
                        for a in range(3)
                    ]
                    for k in range(4):
                        row = [block[META + 4 * k + a : META + 4 * k + a + 1, :] for a in range(3)]
                        g = green(col, row)
                        gh = g.astype(jnp.bfloat16)
                        gl = (g - gh.astype(jnp.float32)).astype(jnp.bfloat16)
                        high[128 * i : 128 * (i + 1), 128 * k : 128 * (k + 1)] = gh
                        low[128 * i : 128 * (i + 1), 128 * k : 128 * (k + 1)] = gl
                both = jnp.dot(high[...], values[...], preferred_element_type=jnp.float32)
                rest = jnp.dot(low[...], values[:, 0:128], preferred_element_type=jnp.float32)
                total[512 * s : 512 * (s + 1), :] += both[:, 0:128] + (both[:, 128:256] + rest)


def near(slots, idx, own_list, sib_list, meta_own, meta_sib, blocks, total):
    first = total is None
    ins = [idx, own_list, sib_list, meta_own, meta_sib, *blocks] + ([] if first else [total])
    return call(
        functools.partial(near_kernel, slots, first),
        f32(1024, 128),
        ins,
        n_smem=3,
        scratch=[
            pltpu.VMEM((512, 256), jnp.bfloat16),
            pltpu.VMEM((256, 128), jnp.float32),
            pltpu.VMEM((512, 512), jnp.bfloat16),
            pltpu.VMEM((512, 512), jnp.bfloat16),
        ],
        flops=len(slots) * 2 * 6 * 512 * 512 * 128,
        nbytes=(1024 * 2 + 512 * len(slots)) * 512,
    )


def quad_kernel(own, bx, by, bd, out):
    part = [
        dot_t(b[EPAIR : EPAIR + 64, :], b[CPAIR : CPAIR + 64, :]) for b in (own, bx, by, bd)
    ]
    out[0:128, :] = part[0] + part[1]
    out[128:256, :] = part[2] + part[3]
    for j, b in enumerate((own, bx, by, bd)):
        out[256 + 32 * j : 288 + 32 * j, :] = b[EQUAD : EQUAD + 32, :]
    out[384:448, :] = own[EPAIR : EPAIR + 64, :]


def top_kernel(idx, mine, theirs, send, ctx, eq_own, eq_oth, coefs):
    device = idx[0]
    core = device % 2
    place = (device // 2) % 4
    for j, eq in enumerate((eq_own, eq_own, eq_oth, eq_oth)):
        parity = (place ^ j) % 2
        mine_at = pl.multiple_of((2 * parity + core) * 32, 32)
        sib_at = pl.multiple_of((2 * parity + 1 - core) * 32, 32)
        eq[pl.ds(mine_at, 32), :] = mine[256 + 32 * j : 288 + 32 * j, :]
        eq[pl.ds(sib_at, 32), :] = theirs[256 + 32 * j : 288 + 32 * j, :]
    quad_own = mine[0:128, :] + theirs[0:128, :]
    quad_oth = mine[128:256, :] + theirs[128:256, :]
    lower = place < 2
    coefs[0:128, :] = jnp.where(lower, quad_own, quad_oth)
    coefs[128:256, :] = jnp.where(lower, quad_oth, quad_own)
    coefs[256:384, :] = dot_t(eq_own[...], quad_own) + dot_t(eq_oth[...], quad_oth)
    coefs[384:512, :] = quad_oth
    half = pl.multiple_of(core * 64, 64)
    for j in range(3):
        send[64 * j : 64 * (j + 1), :] = coefs[pl.ds(128 * j + half, 64), :]
    ctx[0:128, :] = eq_own[...]
    ctx[pl.ds(128 + half, 64), :] = mine[384:448, :]
    ctx[pl.ds(128 + 64 - half, 64), :] = theirs[384:448, :]
    ctx[256:320, :] = coefs[pl.ds(384 + half, 64), :]


def upper_kernel(idx, far_quad, far_top, ctx, r1, r2, r3, skel_quad, skel_top, out, wide, values):
    device = idx[0]
    half = pl.multiple_of((device % 2) * 64, 64)
    plane = device // 8
    quad = device // 4
    received = (r1, r2, r3)
    values[...] = jnp.zeros_like(values)
    bits = window_bits(far_top, plane, 0, FAR_SLOTS, 0)
    cols = columns(skel_top[plane])
    for j, r in enumerate(received):
        other = plane ^ (j + 1)
        values[pl.ds(128 * j + half, 64), :] = r[128:192, :]
        g = green_of(cols, skel_top[other])
        wide[:, 128 * j : 128 * (j + 1)] = jnp.where(has(bits, other), g, 0.0)
    local_top = dot(wide[:, 0:384], values[0:384, :]) * INV_FOUR_PI
    bits = window_bits(far_quad, quad, 0, FAR_SLOTS, quad - 4)
    cols = columns(skel_quad[quad])
    others = [quad ^ 1] + [2 * (plane ^ (j + 1)) + k for j in range(3) for k in range(2)]
    sources = [ctx[256:320, :]] + [r[64 * k : 64 * (k + 1), :] for r in received for k in range(2)]
    for j, (other, source) in enumerate(zip(others, sources)):
        values[pl.ds(128 * j + half, 64), :] = source
        g = green_of(cols, skel_quad[other])
        ok = has(bits, other - quad + 4) & (other >= quad - 4) & (other <= quad + 4)
        wide[:, 128 * j : 128 * (j + 1)] = jnp.where(ok, g, 0.0)
    out[...] = dot(wide[...], values[...]) * INV_FOUR_PI + dot(ctx[0:128, :], local_top)


def lower_kernel(idx, own_list, sib_list, far_pair, ctx, local_quad, meta_sib, skel_pair, *refs):
    blocks = refs[:9]
    out, wide, values = refs[9:]
    device = idx[0]
    core = device % 2
    half = pl.multiple_of(core * 64, 64)
    chips = chips_of(device)
    chip = device // 2
    n_chips = skel_pair.shape[0]
    values[...] = jnp.zeros_like(values)
    bits = window_bits(far_pair, chip, 0, FAR_SLOTS, chip - 4)
    cols = columns(skel_pair[chip])
    for j in range(1, 9):
        other = chips[j]
        values[pl.ds(128 * (j - 1) + half, 64), :] = blocks[j][CPAIR : CPAIR + 64, :]
        g = green_of(cols, skel_pair[jnp.clip(other, 0, n_chips - 1)])
        wide[:, 128 * (j - 1) : 128 * j] = jnp.where(has(bits, other - chip + 4), g, 0.0)
    out[256:384, :] = dot(wide[:, 0:1024], values[0:1024, :]) * INV_FOUR_PI + dot(
        ctx[128:256, :], local_quad[...]
    )
    for j in range(9):
        values[128 * j : 128 * (j + 1), :] = blocks[j][COEF : COEF + 128, :]
    for s, (listed, meta, base) in enumerate(
        ((own_list, blocks[0], META), (sib_list, meta_sib, 64))
    ):
        leaf = device ^ s
        bits = window_bits(listed, 0, NEAR_SLOTS, FAR_SLOTS, leaf - 9)
        skel = jnp.concatenate([meta[base + 4 * a + 3 : base + 4 * a + 4, :] for a in range(3)], axis=0)
        cols = columns(skel)
        for j in range(9):
            b = blocks[j]
            rows = [b[META + 4 * a + 3 : META + 4 * a + 4, :] for a in range(3)]
            g = green([cols[:, a : a + 1] for a in range(3)], rows)
            ok = has(bits, 2 * chips[j] + core - (leaf - 9))
            wide[:, 128 * j : 128 * (j + 1)] = jnp.where(ok, g, 0.0)
        out[128 * s : 128 * (s + 1), :] = dot(wide[...], values[...]) * INV_FOUR_PI


def final_kernel(total, low, got, move, basis, out):
    local_pair = low[256:384, :] + got[640:768, :]
    local = low[0:128, :] + got[512:640, :] + dot(move[0], local_pair)
    out[0] = total[0:512, :] + got[0:512, :] + dot(basis[0], local)


def permute(value, target):
    n = lax.axis_size(AXIS)
    pairs = [(i, target(i)) for i in range(n)]
    return lax.ppermute(value, AXIS, [(i, j) for i, j in pairs if 0 <= j < n and i != j])


def swap(value, mask):
    return permute(value, lambda i: i ^ mask)


def listed_sum(own, entries, skels, coefs):
    def advance(running, partner):
        at = jnp.maximum(partner, 0)
        g = INV_FOUR_PI * green_of(own.T, skels[at])
        contrib = jnp.dot(g, coefs[at], precision=HIGHEST)
        return running + jnp.where(partner >= 0, contrib, 0.0), None

    return lax.scan(advance, jnp.zeros(coefs.shape[1:], jnp.float32), entries)[0]


def upper_anywhere(device, send, ctx, far_quad, far_top, skel_quad, skel_top):
    n = lax.axis_size(AXIS)
    rows = send.shape[0] // 4
    part = lax.dynamic_slice_in_dim(send, (device // 2 % 4) * rows, rows, 0)
    every = lax.all_gather(part, AXIS, axis=0, tiled=True)
    every = every.reshape(n // PLANE, 4, 2, rows, 128).transpose(0, 2, 1, 3, 4)
    every = every.reshape(n // PLANE, 2, 3, 64, 128).transpose(0, 2, 1, 3, 4)
    every = every.reshape(n // PLANE, 3, 128, 128)
    plane, quad = device // 8, device // 4
    local_top = listed_sum(skel_top[plane], far_top[plane], skel_top, every[:, 2])
    quads = every[:, :2].reshape(n // 4, 128, 128)
    far = listed_sum(skel_quad[quad], far_quad[quad], skel_quad, quads)
    whole = far + jnp.dot(ctx[0:128], local_top, precision=HIGHEST)
    return jnp.where(device % 2 == 0, whole, 0.0)


def per_device(
    vectors,
    points,
    leaf_basis,
    transfer_leaf,
    transfer_pair,
    transfer_quad,
    skel_leaf,
    skel_pair,
    skel_quad,
    skel_top,
    near_list,
    far_leaf,
    far_pair,
    far_quad,
    far_top,
):
    n = lax.axis_size(AXIS)
    device = lax.axis_index(AXIS)
    idx = device.reshape(1).astype(jnp.int32)
    own_list = jnp.concatenate([near_list, far_leaf], axis=1)
    sib_list = swap(own_list, 1)

    ship, keep, send = call(
        prepare_kernel,
        (f32(SHIP, 128), f32(64, 128), f32(80, 128)),
        [idx, vectors, points, skel_leaf, leaf_basis, transfer_leaf, transfer_pair, transfer_quad],
        n_smem=1,
        flops=2 * 6 * 640 * 128 * 128,
        nbytes=1 << 20,
    )
    got = swap(send, 1)
    ship = lax.dynamic_update_slice(ship, keep + got[0:64], (CPAIR, 0))

    bd = swap(ship, 6)
    bx = swap(ship, 2)
    by = swap(ship, 4)
    even = swap(ship, 8)
    odd = permute(ship, lambda i: i + 8 if i // 8 % 2 == 1 else i - 8)

    args = (idx, own_list, sib_list, ship[META : META + 16], got[64:80])
    total = near((0,), *args, [ship], None)

    plane_odd = device // 8 % 2 == 1
    place = device // 2 % 4
    crossed = []
    for m in (1, 2):
        lower = (place ^ m) < place
        crossed.append(swap(jnp.where(lower == plane_odd, even[:EPAIR], odd[:EPAIR]), 2 * m))
    cx, cy = crossed
    cd = permute(bd, lambda i: i + 8 if i // 2 % 4 < 2 else i - 8)

    half = call(quad_kernel, f32(448, 128), [ship, bx, by, bd], flops=8 * 6 * 64 * 128 * 128)
    half_got = swap(half, 1)
    up, ctx = call(
        top_kernel,
        (f32(192, 128), f32(320, 128)),
        [idx, half, half_got],
        n_smem=1,
        scratch=[
            pltpu.VMEM((128, 128), jnp.float32),
            pltpu.VMEM((128, 128), jnp.float32),
            pltpu.VMEM((512, 128), jnp.float32),
        ],
        flops=4 * 6 * 128**3,
    )
    if n == 4 * PLANE:
        r1, r2, r3 = [swap(up, PLANE * m) for m in (1, 2, 3)]
        local_quad = call(
            upper_kernel,
            f32(128, 128),
            [idx, far_quad, far_top, ctx, r1, r2, r3, skel_quad, skel_top],
            n_smem=3,
            scratch=[pltpu.VMEM((128, 896), jnp.float32), pltpu.VMEM((896, 128), jnp.float32)],
            flops=2 * 6 * 11 * 128**3,
        )
    else:
        local_quad = upper_anywhere(device, up, ctx, far_quad, far_top, skel_quad, skel_top)

    total = near((1, 2), *args, [bx, by], total)
    total = near((3,), *args, [bd], total)
    total = near((4, 5), *args, [even, odd], total)
    total = near((6, 7), *args, [cx, cy], total)
    total = near((8,), *args, [cd], total)

    low = call(
        lower_kernel,
        f32(384, 128),
        [idx, own_list, sib_list, far_pair, ctx, local_quad, got, skel_pair]
        + [ship, bx, by, bd, even, odd, cx, cy, cd],
        n_smem=4,
        scratch=[pltpu.VMEM((128, 1152), jnp.float32), pltpu.VMEM((1152, 128), jnp.float32)],
        flops=2 * 6 * 28 * 128**3,
    )
    share = swap(jnp.concatenate([total[512:], low[128:]], axis=0), 1)
    return call(
        final_kernel,
        f32(1, 512, 128),
        [total, low, share, transfer_leaf, leaf_basis],
        flops=2 * 6 * 640 * 128 * 128,
    )


def solution(mesh):
    placed = (
        P("leaf", None, None),
        P("leaf", None, None),
        P("leaf", None, None),
        P("leaf", None, None),
        P("leaf", None),
        P("leaf", None),
        P("leaf", None, None),
        P(),
        P(),
        P(),
        P("leaf", None),
        P("leaf", None),
        P(),
        P(),
        P(),
    )
    return jax.shard_map(
        per_device, mesh=mesh, in_specs=placed, out_specs=P("leaf", None, None), check_vma=False
    )
```

```python
import functools

import jax
import jax.numpy as jnp
from jax import lax
from jax.experimental import pallas as pl
from jax.experimental.pallas import tpu as pltpu
from jax.sharding import PartitionSpec as P

INV_FOUR_PI = 0.07957747154594767
DELTA_SQ = 0.01
HIGHEST = lax.Precision.HIGHEST
AXIS = "leaf"

PLANE = 8
NEAR_SLOTS = 16
FAR_SLOTS = 8

META = 0
COEF = 16
PART = 144
PACK = 272
LEAF = 512

VMEM = pl.BlockSpec(memory_space=pltpu.VMEM)
SMEM = pl.BlockSpec(memory_space=pltpu.SMEM)
HBM = pl.BlockSpec(memory_space=pl.ANY)


def call(body, outs, ins, n_smem=0, n_hbm=0, after=(), scratch=(), flops=0, nbytes=0, vmem=32):
    n, m = len(ins), len(after)

    def ordered(*refs):
        return body(*refs[:n], *refs[n + m :])

    return pl.pallas_call(
        ordered if after else body,
        out_shape=outs,
        in_specs=[SMEM] * n_smem + [VMEM] * (n - n_smem - n_hbm) + [HBM] * (n_hbm + m),
        out_specs=jax.tree.map(lambda _: VMEM, outs),
        scratch_shapes=list(scratch),
        compiler_params=pltpu.CompilerParams(vmem_limit_bytes=vmem * 1024 * 1024),
        cost_estimate=pl.CostEstimate(flops=flops, bytes_accessed=nbytes, transcendentals=0),
    )(*ins, *after)


def f32(*shape):
    return jax.ShapeDtypeStruct(shape, jnp.float32)


def dot(a, b):
    return jnp.dot(a, b, precision=HIGHEST, preferred_element_type=jnp.float32)


def dot_t(a, b):
    return lax.dot_general(
        a, b, (((0,), (0,)), ((), ())), precision=HIGHEST, preferred_element_type=jnp.float32
    )


def columns(rows):
    pad = jnp.zeros((128 - rows.shape[0], 128), jnp.float32)
    return jnp.concatenate([rows, pad], axis=0).T


def green(cols, rows):
    dx = cols[0] - rows[0]
    dy = cols[1] - rows[1]
    dz = cols[2] - rows[2]
    return lax.rsqrt((dx * dx + dy * dy) + dz * dz + DELTA_SQ)


def skeleton(skel, cluster):
    return [skel[a, pl.ds(cluster, 1), :] for a in range(3)]


def own_columns(rows):
    cols = columns(jnp.concatenate(rows, axis=0))
    return [cols[:, a : a + 1] for a in range(3)]


def meta_skeleton(ref, at):
    return [ref[at + 4 * a + 3 : at + 4 * a + 4, :] for a in range(3)]


def window_bits(entry_at, count, base):
    bits = jnp.int32(0)
    for e in range(count):
        entry = entry_at(e)
        shift = jnp.clip(entry - base, 0, 31)
        bits = bits | jnp.where(entry >= 0, jnp.left_shift(jnp.int32(1), shift), 0)
    return bits


def leaf_bits(ref, at, start, count, leaf):
    row = ref[at + 15 : at + 16, :].astype(jnp.int32)
    lane = lax.broadcasted_iota(jnp.int32, (1, 128), 1)
    valid = (lane >= start) & (lane < start + count) & (row >= 0)
    shift = jnp.clip(row - (leaf - 9), 0, 23)
    one = jnp.where(valid, jnp.left_shift(jnp.ones_like(row), shift), 0)
    return jnp.sum(one.astype(jnp.float32)).astype(jnp.int32)


def has(bits, place):
    return (jnp.right_shift(bits, jnp.clip(place, 0, 31)) & 1) == 1


def chips_of(device):
    chip = device // 2
    place = chip % 4
    odd = (chip // 4) % 2
    out = [chip, chip ^ 1, chip ^ 2, chip ^ 3, chip ^ 4, chip + jnp.where(odd == 1, 4, -4)]
    for m in (1, 2, 3):
        other = place ^ m
        out.append((chip ^ m) + jnp.where(place < other, -4, 4))
    return out


def prepare_kernel(idx, *refs):
    names = 7
    ins, (ship, keep, send), bufs, sems = refs[:names], refs[names : names + 3], refs[names + 3 : -1], refs[-1]
    copies = [pltpu.make_async_copy(a, b, sems.at[k]) for k, (a, b) in enumerate(zip(ins, bufs))]
    for c in copies:
        c.start()
    for c in copies:
        c.wait()
    vec, basis, move, pts, skel, near_list, far_list = bufs
    core = idx[0] % 2
    pieces = []
    for k in range(4):
        for a in range(3):
            pieces.append(pts[a, :, 128 * k : 128 * (k + 1)])
        if k < 3:
            pieces.append(skel[k])
    rest = jnp.zeros((1, 128 - NEAR_SLOTS - FAR_SLOTS), jnp.float32)
    lists = [near_list[...].astype(jnp.float32), far_list[...].astype(jnp.float32), rest]
    pieces.append(jnp.concatenate(lists, axis=1))
    meta = jnp.concatenate(pieces, axis=0)
    coef = dot_t(basis[0], vec[0])
    up = dot_t(move[0], coef)
    ship[0:LEAF, :] = vec[0]
    ship[LEAF : LEAF + PACK, :] = jnp.concatenate([meta, coef, up], axis=0)
    low, high = up[:64], up[64:]
    keep[...] = jnp.where(core == 0, low, high)
    send[0:64, :] = jnp.where(core == 0, high, low)
    send[64:80, :] = meta


def add_near(device, slots, blocks, metas, total, scratch):
    values, cols, high, low = scratch
    core = device % 2
    chips = chips_of(device)
    bits = []
    for s, (ref, at) in enumerate(metas):
        bits.append(leaf_bits(ref, at, 0, NEAR_SLOTS, device ^ s))
        cols[128 * s : 128 * (s + 1), :] = columns(ref[at : at + 16, :])
    for slot, (vec, pack, at) in zip(slots, blocks):
        leaf = 2 * chips[slot] + core
        v = vec[0:LEAF, :] * INV_FOUR_PI
        vh = v.astype(jnp.bfloat16)
        values[:, 0:128] = vh
        values[:, 128:256] = (v - vh.astype(jnp.float32)).astype(jnp.bfloat16)
        for s in range(2):

            @pl.when(has(bits[s], leaf - ((device ^ s) - 9)))
            def _(pack=pack, at=at, s=s):
                for i in range(4):
                    col = [
                        jnp.broadcast_to(cols[128 * s : 128 * (s + 1), 4 * i + a : 4 * i + a + 1], (128, 128))
                        for a in range(3)
                    ]
                    for k in range(4):
                        row = [pack[at + 4 * k + a : at + 4 * k + a + 1, :] for a in range(3)]
                        g = green(col, row)
                        gh = g.astype(jnp.bfloat16)
                        gl = (g - gh.astype(jnp.float32)).astype(jnp.bfloat16)
                        high[128 * i : 128 * (i + 1), 128 * k : 128 * (k + 1)] = gh
                        low[128 * i : 128 * (i + 1), 128 * k : 128 * (k + 1)] = gl
                both = jnp.dot(high[...], values[...], preferred_element_type=jnp.float32)
                rest = jnp.dot(low[...], values[:, 0:128], preferred_element_type=jnp.float32)
                total[512 * s : 512 * (s + 1), :] += both[:, 0:128] + (both[:, 128:256] + rest)


def add_far(device, slots, blocks, metas, far_pair, skel_pair, out, scratch):
    wide, values = scratch
    n = len(slots)
    core = device % 2
    chips = chips_of(device)
    chip = device // 2
    n_chips = skel_pair.shape[1]
    bits = window_bits(lambda e: far_pair[e, chip], FAR_SLOTS, chip - 4)
    cols = own_columns(skeleton(skel_pair, chip))
    for j, (slot, (_, pack, at)) in enumerate(zip(slots, blocks)):
        other = chips[slot]
        span = slice(128 * j, 128 * (j + 1))
        values[span, :] = pack[at + PART : at + PART + 128, :]
        g = green(cols, skeleton(skel_pair, jnp.clip(other, 0, n_chips - 1)))
        wide[:, span] = jnp.where(has(bits, other - chip + 4), g, 0.0)
    out[256:384, :] += dot(wide[:, 0 : 128 * n], values[0 : 128 * n, :]) * INV_FOUR_PI
    for j, (_, pack, at) in enumerate(blocks):
        values[128 * j : 128 * (j + 1), :] = pack[at + COEF : at + COEF + 128, :]
    for s, (ref, base) in enumerate(metas):
        leaf = device ^ s
        bits = leaf_bits(ref, base, NEAR_SLOTS, FAR_SLOTS, leaf)
        cols = own_columns(meta_skeleton(ref, base))
        for j, (slot, (_, pack, at)) in enumerate(zip(slots, blocks)):
            g = green(cols, meta_skeleton(pack, at))
            ok = has(bits, 2 * chips[slot] + core - (leaf - 9))
            wide[:, 128 * j : 128 * (j + 1)] = jnp.where(ok, g, 0.0)
        out[128 * s : 128 * (s + 1), :] += dot(wide[:, 0 : 128 * n], values[0 : 128 * n, :]) * INV_FOUR_PI


def near_kernel(slots, idx, got, own, *refs):
    n = len(slots)
    if slots == (0,):
        blocks = [(own, own, LEAF)]
        total, *scratch = refs
        total[...] = jnp.zeros_like(total)
    else:
        blocks = [(b, b, LEAF) for b in refs[:n]]
        total_in, total, *scratch = refs[n:]
        total[...] = total_in[...]
    add_near(idx[0], slots, blocks, ((own, LEAF), (got, 64)), total, scratch)


def way_kernel(idx, bx, by, out):
    out[...] = jnp.where(idx[0] % 2 == 0, bx[...], by[...])


def middle_kernel(idx, far_pair, got, own, skel_pair, total_in, bx, by, bd, be, bo, cx, cy, total, low, *scratch):
    total[...] = total_in[...]
    low[...] = jnp.zeros_like(low)
    device = idx[0]
    metas = ((own, LEAF), (got, 64))
    blocks = [(b, b, LEAF) for b in (own, bx, by, bd, be, bo, cx, cy)]
    add_far(device, range(8), blocks, metas, far_pair, skel_pair, low, scratch[4:])
    slots = (3, 6, 7)
    add_near(device, slots, [blocks[j] for j in slots], metas, total, scratch[:4])


def tail_kernel(slots, idx, far_pair, got, own, skel_pair, total_in, low_in, ctx, local_quad, *refs):
    n = len(slots)
    wholes = refs[:n]
    keep, share, *scratch = refs[n:]
    total, low = scratch[6:]
    total[...] = total_in[...]
    low[...] = low_in[...]
    device = idx[0]
    metas = ((own, LEAF), (got, 64))
    blocks = [(b, b, LEAF) for b in wholes]
    add_far(device, slots, blocks, metas, far_pair, skel_pair, low, scratch[4:6])
    low[256:384, :] += dot(ctx[128:256, :], local_quad[...])
    keep[512:640, :] = low[0:128, :]
    keep[640:768, :] = low[256:384, :]
    share[512:768, :] = low[128:384, :]
    add_near(device, slots, blocks, metas, total, scratch[:4])
    keep[0:512, :] = total[0:512, :]
    share[0:512, :] = total[512:1024, :]


def rise_kernel(keep, got, epair, equad, out):
    out[0:128, :] = dot_t(epair[...], keep[...] + got[0:64, :])
    out[128:160, :] = equad[...]


def quad_kernel(own, bx, epair, out):
    out[0:128, :] = own[0:128, :] + bx[0:128, :]
    out[128:160, :] = own[128:160, :]
    out[160:192, :] = bx[128:160, :]
    out[192:256, :] = epair[...]


def top_kernel(idx, mine, theirs, send, ctx, quad, top):
    device = idx[0]
    core = device % 2
    half = pl.multiple_of(core * 64, 64)
    for j in range(2):
        member = 2 * (((device // 2) ^ j) % 2)
        mine_at = pl.multiple_of((member + core) * 32, 32)
        sib_at = pl.multiple_of((member + 1 - core) * 32, 32)
        ctx[pl.ds(mine_at, 32), :] = mine[128 + 32 * j : 160 + 32 * j, :]
        ctx[pl.ds(sib_at, 32), :] = theirs[128 + 32 * j : 160 + 32 * j, :]
    ctx[pl.ds(128 + half, 64), :] = mine[192:256, :]
    ctx[pl.ds(192 - half, 64), :] = theirs[192:256, :]
    quad[...] = mine[0:128, :] + theirs[0:128, :]
    top[...] = dot_t(ctx[0:128, :], quad[...])
    send[0:64, :] = quad[pl.ds(half, 64), :]
    send[64:128, :] = top[pl.ds(half, 64), :]


def join_kernel(mine, theirs, out):
    out[0:64, :] = mine[0:64, :]
    out[64:128, :] = theirs[0:64, :]
    out[128:192, :] = mine[64:128, :] + theirs[64:128, :]


def upper_kernel(idx, far_quad, far_top, ctx, up, r1, r2, r3, skel_quad, skel_top, out, wide, values):
    device = idx[0]
    half = pl.multiple_of((device % 2) * 64, 64)
    plane = device // 8
    quad = device // 4
    received = (r1, r2, r3)
    values[...] = jnp.zeros_like(values)
    bits = window_bits(lambda e: far_top[plane, e], FAR_SLOTS, 0)
    cols = own_columns(skeleton(skel_top, plane))
    for j, r in enumerate(received):
        other = plane ^ (j + 1)
        values[pl.ds(128 * j + half, 64), :] = r[128:192, :]
        g = green(cols, skeleton(skel_top, other))
        wide[:, 128 * j : 128 * (j + 1)] = jnp.where(has(bits, other), g, 0.0)
    local_top = dot(wide[:, 0:384], values[0:384, :]) * INV_FOUR_PI
    bits = window_bits(lambda e: far_quad[quad, e], FAR_SLOTS, quad - 4)
    cols = own_columns(skeleton(skel_quad, quad))
    others = [quad ^ 1] + [(quad ^ (2 * (j + 1))) ^ k for j in range(3) for k in range(2)]
    sources = [up[64:128, :]] + [r[64 * k : 64 * (k + 1), :] for r in received for k in range(2)]
    for j, (other, source) in enumerate(zip(others, sources)):
        values[pl.ds(128 * j + half, 64), :] = source
        g = green(cols, skeleton(skel_quad, other))
        ok = has(bits, other - quad + 4) & (other >= quad - 4) & (other <= quad + 4)
        wide[:, 128 * j : 128 * (j + 1)] = jnp.where(ok, g, 0.0)
    out[...] = dot(wide[...], values[...]) * INV_FOUR_PI + dot(ctx[0:128, :], local_top)


def final_kernel(keep, got, move, basis, out):
    local_pair = keep[640:768, :] + got[640:768, :]
    local = keep[512:640, :] + got[512:640, :] + dot(move[0], local_pair)
    out[0] = keep[0:512, :] + got[0:512, :] + dot(basis[0], local)


def near_scratch():
    return [
        pltpu.VMEM((512, 256), jnp.bfloat16),
        pltpu.VMEM((256, 128), jnp.float32),
        pltpu.VMEM((512, 512), jnp.bfloat16),
        pltpu.VMEM((512, 512), jnp.bfloat16),
    ]


def far_scratch(n):
    return [pltpu.VMEM((128, 128 * n), jnp.float32), pltpu.VMEM((128 * n, 128), jnp.float32)]


NEAR_FLOPS = 2 * 6 * 512 * 512 * 128


def permute(value, target):
    n = lax.axis_size(AXIS)
    pairs = [(i, target(i)) for i in range(n)]
    return lax.ppermute(value, AXIS, [(i, j) for i, j in pairs if 0 <= j < n and i != j])


def swap(value, mask):
    return permute(value, lambda i: i ^ mask)


def listed_sum(own, entries, skels, coefs):
    def advance(running, partner):
        at = jnp.maximum(partner, 0)
        rows = skels[at]
        g = green([own[a][:, None] for a in range(3)], [rows[a][None, :] for a in range(3)]) * INV_FOUR_PI
        contrib = jnp.dot(g, coefs[at], precision=HIGHEST)
        return running + jnp.where(partner >= 0, contrib, 0.0), None

    return lax.scan(advance, jnp.zeros(coefs.shape[1:], jnp.float32), entries)[0]


def upper_anywhere(device, send, ctx, far_quad, far_top, skel_quad, skel_top):
    n = lax.axis_size(AXIS)
    first = jnp.where(device // 4 % 2 == 0, send[0:64], send[64:128])
    second = jnp.where(device // 4 % 2 == 0, send[64:128], send[0:64])
    send = jnp.concatenate([first, second, send[128:192]], axis=0)
    rows = send.shape[0] // 4
    part = lax.dynamic_slice_in_dim(send, (device // 2 % 4) * rows, rows, 0)
    every = lax.all_gather(part, AXIS, axis=0, tiled=True)
    every = every.reshape(n // PLANE, 4, 2, rows, 128).transpose(0, 2, 1, 3, 4)
    every = every.reshape(n // PLANE, 2, 3, 64, 128).transpose(0, 2, 1, 3, 4)
    every = every.reshape(n // PLANE, 3, 128, 128)
    plane, quad = device // 8, device // 4
    local_top = listed_sum(skel_top[plane], far_top[plane], skel_top, every[:, 2])
    quads = every[:, :2].reshape(n // 4, 128, 128)
    far = listed_sum(skel_quad[quad], far_quad[quad], skel_quad, quads)
    whole = far + jnp.dot(ctx[0:128], local_top, precision=HIGHEST)
    return jnp.where(device % 2 == 0, whole, 0.0)


def per_device(
    vectors,
    points,
    leaf_basis,
    transfer_leaf,
    transfer_pair,
    transfer_quad,
    skel_leaf,
    skel_pair,
    skel_quad,
    skel_top,
    near_list,
    far_leaf,
    far_pair,
    far_quad,
    far_top,
):
    n = lax.axis_size(AXIS)
    device = lax.axis_index(AXIS)
    idx = device.reshape(1).astype(jnp.int32)
    def before(i):
        return i + 8 if i // 8 % 2 == 1 else i - 8

    ins = [vectors, leaf_basis, transfer_leaf]
    ins += [points.transpose(1, 0, 2), skel_leaf.transpose(1, 0, 2)]
    ins += [near_list, far_leaf]
    ship, keep, send = call(
        prepare_kernel,
        (f32(LEAF + PACK, 128), f32(64, 128), f32(80, 128)),
        [idx, *ins],
        n_smem=1,
        n_hbm=len(ins),
        scratch=[pltpu.VMEM(a.shape, a.dtype) for a in ins] + [pltpu.SemaphoreType.DMA((len(ins),))],
        flops=2 * 6 * 640 * 128 * 128,
        nbytes=1 << 20,
        vmem=60,
    )
    got = swap(send, 1)
    def near(slots, blocks, total, after):
        return call(
            functools.partial(near_kernel, slots),
            f32(1024, 128),
            [idx, got, ship] + blocks + ([total] if blocks else []),
            n_smem=1,
            after=after,
            scratch=near_scratch(),
            flops=2 * len(slots) * NEAR_FLOPS,
        )

    bx, by, be = [swap(ship, m) for m in (2, 4, 8)]
    bo = permute(ship, before)
    rise = call(rise_kernel, f32(160, 128), [keep, got, transfer_pair, transfer_quad], flops=2 * 6 * 64 * 128 * 128)
    rise_x = swap(rise, 2)
    total = near((0,), [], None, [rise])
    way = call(way_kernel, f32(LEAF + PACK, 128), [idx, bx, by], n_smem=1, after=[total])
    bd = permute(way, lambda i: i ^ 4 if i % 2 == 0 else i ^ 2)

    plane_odd = device // 8 % 2 == 1
    place = device // 2 % 4
    picks = [((place ^ m) < place) == plane_odd for m in (1, 2)]
    cx, cy = [
        swap(jnp.where(pick, be, bo), 2 * m) for m, pick in zip((1, 2), picks)
    ]
    cd = permute(bd, lambda i: i + 8 if i // 2 % 4 < 2 else i - 8)

    half = call(quad_kernel, f32(256, 128), [rise, rise_x, transfer_pair], after=[total])
    half_got = swap(half, 1)
    shared, ctx = call(
        top_kernel,
        (f32(128, 128), f32(256, 128)),
        [idx, half, half_got],
        n_smem=1,
        after=[way],
        scratch=[pltpu.VMEM((128, 128), jnp.float32), pltpu.VMEM((128, 128), jnp.float32)],
        flops=2 * 6 * 128**3,
    )
    total = near((1, 2, 4, 5), [bx, by, be, bo], total, [shared])
    up = call(join_kernel, f32(192, 128), [shared, swap(shared, 4)], after=[total])
    far_pair_t, skel_pair_t = far_pair.T, skel_pair.transpose(1, 0, 2)
    total, low = call(
        middle_kernel,
        (f32(1024, 128), f32(384, 128)),
        [idx, far_pair_t, got, ship, skel_pair_t, total, bx, by, bd, be, bo, cx, cy],
        n_smem=2,
        after=[up],
        scratch=near_scratch() + far_scratch(8),
        flops=6 * NEAR_FLOPS,
    )
    if n == 4 * PLANE:
        received = [swap(up, PLANE * m) for m in (3, 2, 1)]
        skels = [skel_quad.transpose(1, 0, 2), skel_top.transpose(1, 0, 2)]
        local_quad = call(
            upper_kernel,
            f32(128, 128),
            [idx, far_quad, far_top, ctx, up, *received[::-1], *skels],
            n_smem=3,
            after=[low],
            scratch=far_scratch(7),
            flops=2 * 6 * 11 * 128**3,
        )
    else:
        local_quad = upper_anywhere(device, up, ctx, far_quad, far_top, skel_quad, skel_top)

    keep, share = call(
        functools.partial(tail_kernel, (8,)),
        (f32(768, 128), f32(768, 128)),
        [idx, far_pair_t, got, ship, skel_pair_t, total, low, ctx, local_quad, cd],
        n_smem=2,
        scratch=near_scratch()
        + far_scratch(1)
        + [pltpu.VMEM((1024, 128), jnp.float32), pltpu.VMEM((384, 128), jnp.float32)],
        flops=2 * NEAR_FLOPS,
    )
    return call(
        final_kernel,
        f32(1, 512, 128),
        [keep, swap(share, 1), transfer_leaf, leaf_basis],
        flops=2 * 6 * 640 * 128 * 128,
    )


def solution(mesh):
    placed = (
        P("leaf", None, None),
        P("leaf", None, None),
        P("leaf", None, None),
        P("leaf", None, None),
        P("leaf", None),
        P("leaf", None),
        P("leaf", None, None),
        P(),
        P(),
        P(),
        P("leaf", None),
        P("leaf", None),
        P(),
        P(),
        P(),
    )
    return jax.shard_map(
        per_device, mesh=mesh, in_specs=placed, out_specs=P("leaf", None, None), check_vma=False
    )
```

```python
import functools

import jax
import jax.numpy as jnp
from jax import lax
from jax.experimental import pallas as pl
from jax.experimental.pallas import tpu as pltpu
from jax.sharding import PartitionSpec as P

INV_FOUR_PI = 0.07957747154594767
DELTA_SQ = 0.01
HIGHEST = lax.Precision.HIGHEST
AXIS = "leaf"

PLANE = 8
NEAR_SLOTS = 16
FAR_SLOTS = 8

META = 0
COEF = 16
PART = 144
PACK = 272
LEAF = 512
STRIP = 16

VMEM = pl.BlockSpec(memory_space=pltpu.VMEM)
SMEM = pl.BlockSpec(memory_space=pltpu.SMEM)
HBM = pl.BlockSpec(memory_space=pl.ANY)


def call(body, outs, ins, n_smem=0, n_hbm=0, after=(), scratch=(), flops=0, nbytes=0, vmem=32):
    n, m = len(ins), len(after)

    def ordered(*refs):
        return body(*refs[:n], *refs[n + m :])

    return pl.pallas_call(
        ordered if after else body,
        out_shape=outs,
        in_specs=[SMEM] * n_smem + [VMEM] * (n - n_smem - n_hbm) + [HBM] * (n_hbm + m),
        out_specs=jax.tree.map(lambda _: VMEM, outs),
        scratch_shapes=list(scratch),
        compiler_params=pltpu.CompilerParams(vmem_limit_bytes=vmem * 1024 * 1024),
        cost_estimate=pl.CostEstimate(flops=flops, bytes_accessed=nbytes, transcendentals=0),
    )(*ins, *after)


def f32(*shape):
    return jax.ShapeDtypeStruct(shape, jnp.float32)


def dot(a, b):
    return jnp.dot(a, b, precision=HIGHEST, preferred_element_type=jnp.float32)


def dot_t(a, b):
    return lax.dot_general(
        a, b, (((0,), (0,)), ((), ())), precision=HIGHEST, preferred_element_type=jnp.float32
    )


def split(x):
    high = x.astype(jnp.bfloat16)
    return high, (x - high.astype(jnp.float32)).astype(jnp.bfloat16)


def put_values(values, span, x):
    values[span, 0:128], values[span, 128:256] = split(x)


def split_dot(high, low, values):
    both = jnp.dot(high, values, preferred_element_type=jnp.float32)
    rest = jnp.dot(low, values[:, 0:128], preferred_element_type=jnp.float32)
    return both[:, 0:128] + (both[:, 128:256] + rest)


def columns(rows):
    pad = jnp.zeros((128 - rows.shape[0], 128), jnp.float32)
    return jnp.concatenate([rows, pad], axis=0).T


def green(cols, rows):
    dx = cols[0] - rows[0]
    dy = cols[1] - rows[1]
    dz = cols[2] - rows[2]
    return lax.rsqrt((dx * dx + dy * dy) + dz * dz + DELTA_SQ)


def skeleton(skel, cluster):
    return [skel[a, pl.ds(cluster, 1), :] for a in range(3)]


def own_columns(rows):
    cols = columns(jnp.concatenate(rows, axis=0))
    return [cols[:, a : a + 1] for a in range(3)]


def meta_skeleton(ref, at):
    return [ref[at + 4 * a + 3 : at + 4 * a + 4, :] for a in range(3)]


def window_bits(entry_at, count, base):
    bits = jnp.int32(0)
    for e in range(count):
        entry = entry_at(e)
        shift = jnp.clip(entry - base, 0, 31)
        bits = bits | jnp.where(entry >= 0, jnp.left_shift(jnp.int32(1), shift), 0)
    return bits


def leaf_bits(ref, at, start, count, leaf):
    row = ref[at + 15 : at + 16, :].astype(jnp.int32)
    lane = lax.broadcasted_iota(jnp.int32, (1, 128), 1)
    valid = (lane >= start) & (lane < start + count) & (row >= 0)
    shift = jnp.clip(row - (leaf - 9), 0, 23)
    one = jnp.where(valid, jnp.left_shift(jnp.ones_like(row), shift), 0)
    return jnp.sum(one.astype(jnp.float32)).astype(jnp.int32)


def has(bits, place):
    return (jnp.right_shift(bits, jnp.clip(place, 0, 31)) & 1) == 1


def chips_of(device):
    chip = device // 2
    place = chip % 4
    odd = (chip // 4) % 2
    out = [chip, chip ^ 1, chip ^ 2, chip ^ 3, chip ^ 4, chip + jnp.where(odd == 1, 4, -4)]
    for m in (1, 2, 3):
        other = place ^ m
        out.append((chip ^ m) + jnp.where(place < other, -4, 4))
    return out


def prepare_kernel(idx, *refs):
    names = 7
    ins, (ship, keep, send), bufs, sems = refs[:names], refs[names : names + 3], refs[names + 3 : -1], refs[-1]
    copies = [pltpu.make_async_copy(a, b, sems.at[k]) for k, (a, b) in enumerate(zip(ins, bufs))]
    for c in copies:
        c.start()
    for c in copies:
        c.wait()
    vec, basis, move, pts, skel, near_list, far_list = bufs
    core = idx[0] % 2
    pieces = []
    for k in range(4):
        for a in range(3):
            pieces.append(pts[a, :, 128 * k : 128 * (k + 1)])
        if k < 3:
            pieces.append(skel[k])
    rest = jnp.zeros((1, 128 - NEAR_SLOTS - FAR_SLOTS), jnp.float32)
    lists = [near_list[...].astype(jnp.float32), far_list[...].astype(jnp.float32), rest]
    pieces.append(jnp.concatenate(lists, axis=1))
    meta = jnp.concatenate(pieces, axis=0)
    coef = dot_t(basis[0], vec[0])
    up = dot_t(move[0], coef)
    ship[0:LEAF, :] = vec[0]
    ship[LEAF : LEAF + PACK, :] = jnp.concatenate([meta, coef, up], axis=0)
    low, high = up[:64], up[64:]
    keep[...] = jnp.where(core == 0, low, high)
    send[0:64, :] = jnp.where(core == 0, high, low)
    send[64:80, :] = meta


def add_near(device, slots, blocks, metas, total, scratch):
    values, cols = scratch
    core = device % 2
    chips = chips_of(device)
    bits = []
    for s, (ref, at) in enumerate(metas):
        bits.append(leaf_bits(ref, at, 0, NEAR_SLOTS, device ^ s))
        cols[128 * s : 128 * (s + 1), :] = columns(ref[at : at + 16, :])

    def with_sums(*sums):
        for slot, (vec, pack, at) in zip(slots, blocks):
            leaf = 2 * chips[slot] + core
            put_values(values, slice(0, LEAF), vec[0:LEAF, :] * INV_FOUR_PI)
            for s in range(2):
                listed = has(bits[s], leaf - ((device ^ s) - 9))
                for m in range(2):
                    half = values[256 * m : 256 * (m + 1), :]
                    pltpu.matmul_push_rhs(jnp.where(listed, half, jnp.zeros_like(half)), 0, m)
                for i in range(LEAF // STRIP):
                    start, piece = 128 * s + STRIP * i % 128, STRIP * i // 128
                    col = [
                        jnp.broadcast_to(cols[start : start + STRIP, 4 * piece + a : 4 * piece + a + 1], (STRIP, 128))
                        for a in range(3)
                    ]
                    for m in range(2):
                        parts = []
                        for k in (2 * m, 2 * m + 1):
                            row = [pack[at + 4 * k + a : at + 4 * k + a + 1, :] for a in range(3)]
                            parts.append(split(green(col, row)))
                        strip = sums[(s * (LEAF // STRIP) + i) * 2 + m]
                        for j in range(2):
                            side = jnp.concatenate([part[j] for part in parts], axis=1)
                            pltpu.matmul_acc_lhs(strip, side, 0 if i == 0 and j == 0 else None)
        for i in range(2 * LEAF // STRIP):
            both = pltpu.matmul_pop(sums[2 * i]) + pltpu.matmul_pop(sums[2 * i + 1])
            total[STRIP * i : STRIP * (i + 1), :] += both[:, 0:128] + both[:, 128:256]

    shape = (STRIP, 256)
    pl.run_scoped(with_sums, *[pltpu.ACC(m)(shape, jnp.float32) for _ in range(2 * LEAF // STRIP) for m in range(2)])


def add_far(device, slots, blocks, metas, far_pair, skel_pair, out, scratch):
    high, low, values = scratch
    n = len(slots)
    core = device % 2
    chips = chips_of(device)
    chip = device // 2
    n_chips = skel_pair.shape[1]
    depth = slice(0, 128 * n)
    bits = window_bits(lambda e: far_pair[e, chip], FAR_SLOTS, chip - 4)
    cols = own_columns(skeleton(skel_pair, chip))
    for j, (slot, (_, pack, at)) in enumerate(zip(slots, blocks)):
        other = chips[slot]
        span = slice(128 * j, 128 * (j + 1))
        put_values(values, span, pack[at + PART : at + PART + 128, :])
        g = green(cols, skeleton(skel_pair, jnp.clip(other, 0, n_chips - 1)))
        high[0:128, span], low[0:128, span] = split(jnp.where(has(bits, other - chip + 4), g, 0.0))
    out[256:384, :] += split_dot(high[0:128, depth], low[0:128, depth], values[depth, :]) * INV_FOUR_PI
    for j, (_, pack, at) in enumerate(blocks):
        put_values(values, slice(128 * j, 128 * (j + 1)), pack[at + COEF : at + COEF + 128, :])
    for s, (ref, base) in enumerate(metas):
        leaf = device ^ s
        bits = leaf_bits(ref, base, NEAR_SLOTS, FAR_SLOTS, leaf)
        cols = own_columns(meta_skeleton(ref, base))
        for j, (slot, (_, pack, at)) in enumerate(zip(slots, blocks)):
            g = green(cols, meta_skeleton(pack, at))
            ok = has(bits, 2 * chips[slot] + core - (leaf - 9))
            here = (slice(128 * s, 128 * (s + 1)), slice(128 * j, 128 * (j + 1)))
            high[here], low[here] = split(jnp.where(ok, g, 0.0))
    out[0:256, :] += split_dot(high[:, depth], low[:, depth], values[depth, :]) * INV_FOUR_PI


def own_kernel(idx, got, ship, total, own, *scratch):
    copy = pltpu.make_async_copy(ship, own, scratch[-1])
    copy.start()
    total[...] = jnp.zeros_like(total)
    copy.wait()
    add_near(idx[0], (0,), [(own, own, LEAF)], ((own, LEAF), (got, 64)), total, scratch[:-1])


def near_kernel(slots, idx, got, own, *refs):
    n = len(slots)
    blocks = [(b, b, LEAF) for b in refs[:n]]
    total_in, total, *scratch = refs[n:]
    total[...] = total_in[...]
    add_near(idx[0], slots, blocks, ((own, LEAF), (got, 64)), total, scratch)


def stack_kernel(*refs):
    out = refs[-1]
    for j, r in enumerate(refs[:-1]):
        out[128 * j : 128 * (j + 1), :] = r[...]


def cross_kernel(idx, even, odd, *outs):
    plane_odd = idx[0] // 8 % 2 == 1
    place = idx[0] // 2 % 4
    for m, out in zip((1, 2), outs):
        out[...] = jnp.where(((place ^ m) < place) == plane_odd, even[...], odd[...])


def way_kernel(idx, bx, by, out):
    out[...] = jnp.where(idx[0] % 2 == 0, bx[...], by[...])


def close_kernel(idx, far_pair, got, own, skel_pair, total, ctx, quad_own, quad_got, *refs):
    blocks = [(b, b, LEAF) for b in (own,) + refs[:8]]
    keep, share, low, *scratch = refs[8:]
    low[...] = jnp.zeros_like(low)
    add_far(idx[0], range(9), blocks, ((own, LEAF), (got, 64)), far_pair, skel_pair, low, scratch)
    local_top = quad_own[128:256, :] + quad_got[128:256, :]
    local_quad = quad_own[0:128, :] + quad_got[0:128, :] + dot(ctx[0:128, :], local_top)
    low[256:384, :] += dot(ctx[128:256, :], local_quad)
    keep[0:512, :] = total[0:512, :]
    keep[512:640, :] = low[0:128, :]
    keep[640:768, :] = low[256:384, :]
    share[0:512, :] = total[512:1024, :]
    share[512:768, :] = low[128:384, :]


def rise_kernel(keep, got, epair, equad, out, moved):
    moved[...] = epair[...]
    out[0:128, :] = dot_t(epair[...], keep[...] + got[0:64, :])
    out[128:160, :] = equad[...]


def quad_kernel(own, bx, epair, out):
    out[0:128, :] = own[0:128, :] + bx[0:128, :]
    out[128:160, :] = own[128:160, :]
    out[160:192, :] = bx[128:160, :]
    out[192:256, :] = epair[...]


def top_kernel(idx, mine, theirs, send, ctx, quad, top):
    device = idx[0]
    core = device % 2
    half = pl.multiple_of(core * 64, 64)
    for j in range(2):
        member = 2 * (((device // 2) ^ j) % 2)
        mine_at = pl.multiple_of((member + core) * 32, 32)
        sib_at = pl.multiple_of((member + 1 - core) * 32, 32)
        ctx[pl.ds(mine_at, 32), :] = mine[128 + 32 * j : 160 + 32 * j, :]
        ctx[pl.ds(sib_at, 32), :] = theirs[128 + 32 * j : 160 + 32 * j, :]
    ctx[pl.ds(128 + half, 64), :] = mine[192:256, :]
    ctx[pl.ds(192 - half, 64), :] = theirs[192:256, :]
    quad[...] = mine[0:128, :] + theirs[0:128, :]
    top[...] = dot_t(ctx[0:128, :], quad[...])
    send[0:64, :] = quad[pl.ds(half, 64), :]
    send[64:128, :] = top[pl.ds(half, 64), :]


def upper_kernel(idx, far_quad, far_top, planes, skel_quad, skel_top, mine, send, high, low, values, rows):
    device = idx[0]
    half = pl.multiple_of((device % 2) * 64, 64)
    plane = device // 8
    quad = device // 4
    rows[...] = jnp.zeros_like(rows)
    for j in range(4):
        rows[pl.ds(128 * j + half, 64), :] = planes[128 * j + 64 : 128 * (j + 1), :]
    put_values(values, slice(0, 512), rows[...])
    bits = window_bits(lambda e: far_top[plane, e], FAR_SLOTS, 0)
    cols = own_columns(skeleton(skel_top, plane))
    for j in range(4):
        other = plane ^ j
        span = slice(128 * j, 128 * (j + 1))
        g = jnp.where(has(bits, other), green(cols, skeleton(skel_top, other)), 0.0)
        high[0:128, span], low[0:128, span] = split(g)
    top = split_dot(high[0:128, :], low[0:128, :], values[...]) * INV_FOUR_PI
    mine[128:256, :] = top
    send[128:256, :] = top
    for j in range(4):
        rows[pl.ds(128 * j + half, 64), :] = planes[128 * j : 128 * j + 64, :]
    put_values(values, slice(0, 512), rows[...])
    for s in range(2):
        target = quad ^ s
        bits = window_bits(lambda e: far_quad[target, e], FAR_SLOTS, target - 4)
        cols = own_columns(skeleton(skel_quad, target))
        for j in range(4):
            other = quad ^ (2 * j)
            here = (slice(128 * s, 128 * (s + 1)), slice(128 * j, 128 * (j + 1)))
            ok = has(bits, other - target + 4) & (other >= target - 4) & (other <= target + 4)
            high[here], low[here] = split(jnp.where(ok, green(cols, skeleton(skel_quad, other)), 0.0))
    far = split_dot(high[...], low[...], values[...]) * INV_FOUR_PI
    mine[0:128, :] = far[0:128]
    send[0:128, :] = far[128:256]


def final_kernel(keep, got, move, basis, out):
    local_pair = keep[640:768, :] + got[640:768, :]
    local = keep[512:640, :] + got[512:640, :] + dot(move[0], local_pair)
    out[0] = keep[0:512, :] + got[0:512, :] + dot(basis[0], local)


def near_scratch():
    return [
        pltpu.VMEM((512, 256), jnp.bfloat16),
        pltpu.VMEM((256, 128), jnp.float32),
    ]


def far_scratch(rows, n):
    wide = pltpu.VMEM((rows, 128 * n), jnp.bfloat16)
    return [wide, wide, pltpu.VMEM((128 * n, 256), jnp.bfloat16)]


NEAR_FLOPS = 2 * 6 * 512 * 512 * 128


def permute(value, target):
    n = lax.axis_size(AXIS)
    pairs = [(i, target(i)) for i in range(n)]
    return lax.ppermute(value, AXIS, [(i, j) for i, j in pairs if 0 <= j < n and i != j])


def swap(value, mask):
    return permute(value, lambda i: i ^ mask)


def listed_sum(own, entries, skels, coefs):
    def advance(running, partner):
        at = jnp.maximum(partner, 0)
        rows = skels[at]
        g = green([own[a][:, None] for a in range(3)], [rows[a][None, :] for a in range(3)]) * INV_FOUR_PI
        contrib = jnp.dot(g, coefs[at], precision=HIGHEST)
        return running + jnp.where(partner >= 0, contrib, 0.0), None

    return lax.scan(advance, jnp.zeros(coefs.shape[1:], jnp.float32), entries)[0]


def upper_anywhere(device, send, ctx, far_quad, far_top, skel_quad, skel_top):
    n = lax.axis_size(AXIS)
    part = lax.dynamic_slice_in_dim(send, device // 2 % 2 * 64, 64, 0)
    every = lax.all_gather(part, AXIS, axis=0, tiled=True).reshape(n // 4, 2, 2, 64, 128)
    quads = every[:, 0].reshape(n // 4, 128, 128)
    tops = every[:, 1].reshape(n // PLANE, 2, 128, 128).sum(axis=1)
    plane, quad = device // 8, device // 4
    local_top = listed_sum(skel_top[plane], far_top[plane], skel_top, tops)
    far = listed_sum(skel_quad[quad], far_quad[quad], skel_quad, quads)
    whole = jnp.concatenate([far, local_top], axis=0)
    return jnp.where(device % 2 == 0, whole, 0.0)


def per_device(
    vectors,
    points,
    leaf_basis,
    transfer_leaf,
    transfer_pair,
    transfer_quad,
    skel_leaf,
    skel_pair,
    skel_quad,
    skel_top,
    near_list,
    far_leaf,
    far_pair,
    far_quad,
    far_top,
):
    n = lax.axis_size(AXIS)
    device = lax.axis_index(AXIS)
    idx = device.reshape(1).astype(jnp.int32)
    def before(i):
        return i + 8 if i // 8 % 2 == 1 else i - 8

    ins = [vectors, leaf_basis, transfer_leaf]
    ins += [points.transpose(1, 0, 2), skel_leaf.transpose(1, 0, 2)]
    ins += [near_list, far_leaf]
    ship, keep, send = call(
        prepare_kernel,
        (f32(LEAF + PACK, 128), f32(64, 128), f32(80, 128)),
        [idx, *ins],
        n_smem=1,
        n_hbm=len(ins),
        scratch=[pltpu.VMEM(a.shape, a.dtype) for a in ins] + [pltpu.SemaphoreType.DMA((len(ins),))],
        flops=2 * 6 * 640 * 128 * 128,
        nbytes=1 << 20,
        vmem=60,
    )
    got = swap(send, 1)
    def near(slots, blocks, total, after):
        return call(
            functools.partial(near_kernel, slots),
            f32(1024, 128),
            [idx, got, own] + blocks + [total],
            n_smem=1,
            after=after,
            scratch=near_scratch(),
            flops=2 * len(slots) * NEAR_FLOPS,
        )

    bx, by, be = [swap(ship, m) for m in (2, 4, 8)]
    bo = permute(ship, before)
    rise, epair = call(rise_kernel, (f32(160, 128), f32(64, 128)), [keep, got, transfer_pair, transfer_quad], flops=2 * 6 * 64 * 128 * 128)
    rise_x = swap(rise, 2)
    total, own = call(
        own_kernel,
        (f32(1024, 128), f32(LEAF + PACK, 128)),
        [idx, got, ship],
        n_smem=1,
        n_hbm=1,
        after=[rise],
        scratch=near_scratch() + [pltpu.SemaphoreType.DMA],
        flops=2 * NEAR_FLOPS,
    )
    half = call(quad_kernel, f32(256, 128), [rise, rise_x, epair], after=[total])
    way = call(way_kernel, f32(LEAF + PACK, 128), [idx, bx, by], n_smem=1, after=[half])
    bd = permute(way, lambda i: i ^ 4 if i % 2 == 0 else i ^ 2)

    half_got = swap(half, 1)
    shared, ctx = call(
        top_kernel,
        (f32(128, 128), f32(256, 128)),
        [idx, half, half_got],
        n_smem=1,
        after=[way],
        scratch=[pltpu.VMEM((128, 128), jnp.float32), pltpu.VMEM((128, 128), jnp.float32)],
        flops=2 * 6 * 128**3,
    )
    direct = n == 4 * PLANE
    received = [swap(shared, PLANE * m) for m in (3, 2, 1)][::-1] if direct else []
    block = f32(LEAF + PACK, 128)
    sx, sy = call(cross_kernel, (block,) * 2, [idx, be, bo], n_smem=1, after=[shared])
    cx, cy = swap(sx, 2), swap(sy, 4)
    cd = permute(bd, lambda i: i + 8 if i // 2 % 4 < 2 else i - 8)
    total = near((1, 2), [bx, by], total, [sx])
    total = near((4, 5), [be, bo], total, [])
    planes = call(stack_kernel, f32(512, 128), [shared, *received], after=[total]) if direct else shared
    if direct:
        skels = [skel_quad.transpose(1, 0, 2), skel_top.transpose(1, 0, 2)]
        quad_own, quad_send = call(
            upper_kernel,
            (f32(256, 128), f32(256, 128)),
            [idx, far_quad, far_top, planes, *skels],
            n_smem=3,
            after=[total],
            scratch=far_scratch(256, 4) + [pltpu.VMEM((512, 128), jnp.float32)],
            flops=2 * 6 * 12 * 128**3,
        )
        quad_got = swap(quad_send, 4)
    else:
        quad_own = upper_anywhere(device, shared, ctx, far_quad, far_top, skel_quad, skel_top)
        quad_got = jnp.zeros_like(quad_own)
    far_pair_t, skel_pair_t = far_pair.T, skel_pair.transpose(1, 0, 2)
    total = near((3, 6, 7), [bd, cx, cy], total, [quad_own])
    total = near((8,), [cd], total, [])
    keep, share = call(
        close_kernel,
        (f32(768, 128), f32(768, 128)),
        [idx, far_pair_t, got, own, skel_pair_t, total, ctx, quad_own, quad_got]
        + [bx, by, bd, be, bo, cx, cy, cd],
        n_smem=2,
        scratch=[pltpu.VMEM((384, 128), jnp.float32)] + far_scratch(256, 9),
        flops=2 * 3 * 28 * 128**3,
    )
    return call(
        final_kernel,
        f32(1, 512, 128),
        [keep, swap(share, 1), transfer_leaf, leaf_basis],
        flops=2 * 6 * 640 * 128 * 128,
    )


def solution(mesh):
    placed = (
        P("leaf", None, None),
        P("leaf", None, None),
        P("leaf", None, None),
        P("leaf", None, None),
        P("leaf", None),
        P("leaf", None),
        P("leaf", None, None),
        P(),
        P(),
        P(),
        P("leaf", None),
        P("leaf", None),
        P(),
        P(),
        P(),
    )
    return jax.shard_map(
        per_device, mesh=mesh, in_specs=placed, out_specs=P("leaf", None, None), check_vma=False
    )
```

```python
import functools

import jax
import jax.numpy as jnp
from jax import lax
from jax.experimental import pallas as pl
from jax.experimental.pallas import tpu as pltpu
from jax.sharding import PartitionSpec as P

INV_FOUR_PI = 0.07957747154594767
DELTA_SQ = 0.01
HIGHEST = lax.Precision.HIGHEST
AXIS = "leaf"

PLANE = 8
NEAR_SLOTS = 16
FAR_SLOTS = 8

META = 0
COEF = 16
PART = 144
PACK = 272
LEAF = 512
STRIP = 16

VMEM = pl.BlockSpec(memory_space=pltpu.VMEM)
SMEM = pl.BlockSpec(memory_space=pltpu.SMEM)
HBM = pl.BlockSpec(memory_space=pl.ANY)


def call(body, outs, ins, n_smem=0, n_hbm=0, after=(), scratch=(), flops=0, nbytes=0, vmem=32):
    n, m = len(ins), len(after)

    def ordered(*refs):
        return body(*refs[:n], *refs[n + m :])

    return pl.pallas_call(
        ordered if after else body,
        out_shape=outs,
        in_specs=[SMEM] * n_smem + [VMEM] * (n - n_smem - n_hbm) + [HBM] * (n_hbm + m),
        out_specs=jax.tree.map(lambda _: VMEM, outs),
        scratch_shapes=list(scratch),
        compiler_params=pltpu.CompilerParams(vmem_limit_bytes=vmem * 1024 * 1024),
        cost_estimate=pl.CostEstimate(flops=flops, bytes_accessed=nbytes, transcendentals=0),
    )(*ins, *after)


def f32(*shape):
    return jax.ShapeDtypeStruct(shape, jnp.float32)


def dot(a, b):
    return jnp.dot(a, b, precision=HIGHEST, preferred_element_type=jnp.float32)


def dot_t(a, b):
    return lax.dot_general(
        a, b, (((0,), (0,)), ((), ())), precision=HIGHEST, preferred_element_type=jnp.float32
    )


def split(x):
    high = x.astype(jnp.bfloat16)
    return high, (x - high.astype(jnp.float32)).astype(jnp.bfloat16)


def put_values(values, span, x):
    values[span, 0:128], values[span, 128:256] = split(x)


def split_dot(high, low, values):
    both = jnp.dot(high, values, preferred_element_type=jnp.float32)
    rest = jnp.dot(low, values[:, 0:128], preferred_element_type=jnp.float32)
    return both[:, 0:128] + (both[:, 128:256] + rest)


def three_dot(a, b, contract=1):
    (ah, al), (bh, bl) = split(a), split(b)

    def one(x, y):
        return lax.dot_general(x, y, (((contract,), (0,)), ((), ())), preferred_element_type=jnp.float32)

    return one(ah, bh) + (one(ah, bl) + one(al, bh))


def columns(rows):
    pad = jnp.zeros((128 - rows.shape[0], 128), jnp.float32)
    return jnp.concatenate([rows, pad], axis=0).T


def green(cols, rows):
    dx = cols[0] - rows[0]
    dy = cols[1] - rows[1]
    dz = cols[2] - rows[2]
    return lax.rsqrt((dx * dx + dy * dy) + dz * dz + DELTA_SQ)


def skeleton(skel, cluster):
    return [skel[a, pl.ds(cluster, 1), :] for a in range(3)]


def own_columns(rows):
    cols = columns(jnp.concatenate(rows, axis=0))
    return [cols[:, a : a + 1] for a in range(3)]


def meta_skeleton(ref, at):
    return [ref[at + 4 * a + 3 : at + 4 * a + 4, :] for a in range(3)]


def window_bits(entry_at, count, base):
    bits = jnp.int32(0)
    for e in range(count):
        entry = entry_at(e)
        shift = jnp.clip(entry - base, 0, 31)
        bits = bits | jnp.where(entry >= 0, jnp.left_shift(jnp.int32(1), shift), 0)
    return bits


def leaf_bits(ref, at, start, count, leaf):
    row = ref[at + 15 : at + 16, :].astype(jnp.int32)
    lane = lax.broadcasted_iota(jnp.int32, (1, 128), 1)
    valid = (lane >= start) & (lane < start + count) & (row >= 0)
    shift = jnp.clip(row - (leaf - 9), 0, 23)
    one = jnp.where(valid, jnp.left_shift(jnp.ones_like(row), shift), 0)
    return jnp.sum(one.astype(jnp.float32)).astype(jnp.int32)


def has(bits, place):
    return (jnp.right_shift(bits, jnp.clip(place, 0, 31)) & 1) == 1


def chips_of(device):
    chip = device // 2
    place = chip % 4
    odd = (chip // 4) % 2
    out = [chip, chip ^ 1, chip ^ 2, chip ^ 3, chip ^ 4, chip + jnp.where(odd == 1, 4, -4)]
    for m in (1, 2, 3):
        other = place ^ m
        out.append((chip ^ m) + jnp.where(place < other, -4, 4))
    return out


def prepare_kernel(idx, *refs):
    names = 7
    ins, (ship, keep, send), bufs, sems = refs[:names], refs[names : names + 3], refs[names + 3 : -1], refs[-1]
    copies = [pltpu.make_async_copy(a, b, sems.at[k]) for k, (a, b) in enumerate(zip(ins, bufs))]
    for c in copies:
        c.start()
    for c in copies:
        c.wait()
    vec, basis, move, pts, skel, near_list, far_list = bufs
    core = idx[0] % 2
    pieces = []
    for k in range(4):
        for a in range(3):
            pieces.append(pts[a, :, 128 * k : 128 * (k + 1)])
        if k < 3:
            pieces.append(skel[k])
    rest = jnp.zeros((1, 128 - NEAR_SLOTS - FAR_SLOTS), jnp.float32)
    lists = [near_list[...].astype(jnp.float32), far_list[...].astype(jnp.float32), rest]
    pieces.append(jnp.concatenate(lists, axis=1))
    meta = jnp.concatenate(pieces, axis=0)
    coef = three_dot(basis[0], vec[0], 0)
    up = three_dot(move[0], coef, 0)
    ship[0:LEAF, :] = vec[0]
    ship[LEAF : LEAF + PACK, :] = jnp.concatenate([meta, coef, up], axis=0)
    low, high = up[:64], up[64:]
    keep[...] = jnp.where(core == 0, low, high)
    send[0:64, :] = jnp.where(core == 0, high, low)
    send[64:80, :] = meta


def add_near(device, slots, blocks, metas, total, scratch):
    values, cols = scratch
    core = device % 2
    chips = chips_of(device)
    bits = []
    for s, (ref, at) in enumerate(metas):
        bits.append(leaf_bits(ref, at, 0, NEAR_SLOTS, device ^ s))
        cols[128 * s : 128 * (s + 1), :] = columns(ref[at : at + 16, :])

    def with_sums(*sums):
        for slot, (vec, pack, at) in zip(slots, blocks):
            leaf = 2 * chips[slot] + core
            put_values(values, slice(0, LEAF), vec[0:LEAF, :] * INV_FOUR_PI)
            for s in range(2):
                listed = has(bits[s], leaf - ((device ^ s) - 9))
                for m in range(2):
                    half = values[256 * m : 256 * (m + 1), :]
                    pltpu.matmul_push_rhs(jnp.where(listed, half, jnp.zeros_like(half)), 0, m)
                for i in range(LEAF // STRIP):
                    start, piece = 128 * s + STRIP * i % 128, STRIP * i // 128
                    col = [
                        jnp.broadcast_to(cols[start : start + STRIP, 4 * piece + a : 4 * piece + a + 1], (STRIP, 128))
                        for a in range(3)
                    ]
                    for m in range(2):
                        parts = []
                        for k in (2 * m, 2 * m + 1):
                            row = [pack[at + 4 * k + a : at + 4 * k + a + 1, :] for a in range(3)]
                            parts.append(split(green(col, row)))
                        strip = sums[(s * (LEAF // STRIP) + i) * 2 + m]
                        for j in range(2):
                            side = jnp.concatenate([part[j] for part in parts], axis=1)
                            pltpu.matmul_acc_lhs(strip, side, 0 if i == 0 and j == 0 else None)
        for i in range(2 * LEAF // STRIP):
            both = pltpu.matmul_pop(sums[2 * i]) + pltpu.matmul_pop(sums[2 * i + 1])
            total[STRIP * i : STRIP * (i + 1), :] += both[:, 0:128] + both[:, 128:256]

    shape = (STRIP, 256)
    pl.run_scoped(with_sums, *[pltpu.ACC(m)(shape, jnp.float32) for _ in range(2 * LEAF // STRIP) for m in range(2)])


def add_far(device, slots, blocks, metas, far_pair, skel_pair, out, scratch):
    high, low, values = scratch
    n = len(slots)
    core = device % 2
    chips = chips_of(device)
    chip = device // 2
    n_chips = skel_pair.shape[1]
    depth = slice(0, 128 * n)
    bits = window_bits(lambda e: far_pair[e, chip], FAR_SLOTS, chip - 4)
    cols = own_columns(skeleton(skel_pair, chip))
    for j, (slot, (_, pack, at)) in enumerate(zip(slots, blocks)):
        other = chips[slot]
        span = slice(128 * j, 128 * (j + 1))
        put_values(values, span, pack[at + PART : at + PART + 128, :])
        g = green(cols, skeleton(skel_pair, jnp.clip(other, 0, n_chips - 1)))
        high[0:128, span], low[0:128, span] = split(jnp.where(has(bits, other - chip + 4), g, 0.0))
    out[256:384, :] += split_dot(high[0:128, depth], low[0:128, depth], values[depth, :]) * INV_FOUR_PI
    for j, (_, pack, at) in enumerate(blocks):
        put_values(values, slice(128 * j, 128 * (j + 1)), pack[at + COEF : at + COEF + 128, :])
    for s, (ref, base) in enumerate(metas):
        leaf = device ^ s
        bits = leaf_bits(ref, base, NEAR_SLOTS, FAR_SLOTS, leaf)
        cols = own_columns(meta_skeleton(ref, base))
        for j, (slot, (_, pack, at)) in enumerate(zip(slots, blocks)):
            g = green(cols, meta_skeleton(pack, at))
            ok = has(bits, 2 * chips[slot] + core - (leaf - 9))
            here = (slice(128 * s, 128 * (s + 1)), slice(128 * j, 128 * (j + 1)))
            high[here], low[here] = split(jnp.where(ok, g, 0.0))
    out[0:256, :] += split_dot(high[:, depth], low[:, depth], values[depth, :]) * INV_FOUR_PI


def own_kernel(idx, got, ship, total, own, *scratch):
    copy = pltpu.make_async_copy(ship, own, scratch[-1])
    copy.start()
    total[...] = jnp.zeros_like(total)
    copy.wait()
    add_near(idx[0], (0,), [(own, own, LEAF)], ((own, LEAF), (got, 64)), total, scratch[:-1])


def near_kernel(slots, idx, got, own, *refs):
    n = len(slots)
    blocks = [(b, b, LEAF) for b in refs[:n]]
    total_in, total, *scratch = refs[n:]
    total[...] = total_in[...]
    add_near(idx[0], slots, blocks, ((own, LEAF), (got, 64)), total, scratch)


def stack_kernel(*refs):
    out = refs[-1]
    for j, r in enumerate(refs[:-1]):
        out[128 * j : 128 * (j + 1), :] = r[...]


def cross_kernel(idx, even, odd, *outs):
    plane_odd = idx[0] // 8 % 2 == 1
    place = idx[0] // 2 % 4
    for m, out in zip((1, 2), outs):
        out[...] = jnp.where(((place ^ m) < place) == plane_odd, even[...], odd[...])


def fetch_kernel(*refs):
    half = len(refs) // 2
    for a, b in zip(refs[:half], refs[half:]):
        b[...] = a[...]


def way_kernel(idx, bx, by, out):
    out[...] = jnp.where(idx[0] % 2 == 0, bx[...], by[...])


def last_kernel(slots, idx, got, own, block, total_in, mine, share, total, *scratch):
    total[...] = total_in[...]
    add_near(idx[0], slots, [(block, block, LEAF)], ((own, LEAF), (got, 64)), total, scratch)
    mine[...] = total[0:512, :]
    share[...] = total[512:1024, :]


def close_kernel(idx, far_pair, got, own, skel_pair, ctx, quad_own, quad_got, *refs):
    blocks = [(b, b, LEAF) for b in (own,) + refs[:8]]
    keep, share, low, *scratch = refs[8:]
    low[...] = jnp.zeros_like(low)
    add_far(idx[0], range(9), blocks, ((own, LEAF), (got, 64)), far_pair, skel_pair, low, scratch)
    local_top = quad_own[128:256, :] + quad_got[128:256, :]
    local_quad = quad_own[0:128, :] + quad_got[0:128, :] + dot(ctx[0:128, :], local_top)
    low[256:384, :] += dot(ctx[128:256, :], local_quad)
    keep[0:128, :] = low[0:128, :]
    keep[128:256, :] = low[256:384, :]
    share[...] = low[128:384, :]


def rise_kernel(keep, got, epair, equad, out, moved):
    moved[...] = epair[...]
    out[0:128, :] = dot_t(epair[...], keep[...] + got[0:64, :])
    out[128:160, :] = equad[...]


def quad_kernel(own, bx, epair, out):
    out[0:128, :] = own[0:128, :] + bx[0:128, :]
    out[128:160, :] = own[128:160, :]
    out[160:192, :] = bx[128:160, :]
    out[192:256, :] = epair[...]


def top_kernel(idx, mine, theirs, send, ctx, quad, top):
    device = idx[0]
    core = device % 2
    half = pl.multiple_of(core * 64, 64)
    for j in range(2):
        member = 2 * (((device // 2) ^ j) % 2)
        mine_at = pl.multiple_of((member + core) * 32, 32)
        sib_at = pl.multiple_of((member + 1 - core) * 32, 32)
        ctx[pl.ds(mine_at, 32), :] = mine[128 + 32 * j : 160 + 32 * j, :]
        ctx[pl.ds(sib_at, 32), :] = theirs[128 + 32 * j : 160 + 32 * j, :]
    ctx[pl.ds(128 + half, 64), :] = mine[192:256, :]
    ctx[pl.ds(192 - half, 64), :] = theirs[192:256, :]
    quad[...] = mine[0:128, :] + theirs[0:128, :]
    top[...] = dot_t(ctx[0:128, :], quad[...])
    send[0:64, :] = quad[pl.ds(half, 64), :]
    send[64:128, :] = top[pl.ds(half, 64), :]


def upper_kernel(idx, far_quad, far_top, two, others, skel_quad, skel_top, mine, send, high, low, values, rows):
    device = idx[0]
    half = pl.multiple_of((device % 2) * 64, 64)
    plane = device // 8
    quad = device // 4
    rows[...] = jnp.zeros_like(rows)
    for j in range(4):
        at = 128 * (j % 2)
        rows[pl.ds(128 * j + half, 64), :] = (two, others)[j // 2][at + 64 : at + 128, :]
    put_values(values, slice(0, 512), rows[...])
    bits = window_bits(lambda e: far_top[plane, e], FAR_SLOTS, 0)
    cols = own_columns(skeleton(skel_top, plane))
    for j in range(4):
        other = plane ^ j
        span = slice(128 * j, 128 * (j + 1))
        g = jnp.where(has(bits, other), green(cols, skeleton(skel_top, other)), 0.0)
        high[0:128, span], low[0:128, span] = split(g)
    top = split_dot(high[0:128, :], low[0:128, :], values[...]) * INV_FOUR_PI
    mine[128:256, :] = top
    send[128:256, :] = top
    for j in range(4):
        at = 128 * (j % 2)
        rows[pl.ds(128 * j + half, 64), :] = (two, others)[j // 2][at : at + 64, :]
    put_values(values, slice(0, 512), rows[...])
    for s in range(2):
        target = quad ^ s
        bits = window_bits(lambda e: far_quad[target, e], FAR_SLOTS, target - 4)
        cols = own_columns(skeleton(skel_quad, target))
        for j in range(4):
            other = quad ^ (2 * j)
            here = (slice(128 * s, 128 * (s + 1)), slice(128 * j, 128 * (j + 1)))
            ok = has(bits, other - target + 4) & (other >= target - 4) & (other <= target + 4)
            high[here], low[here] = split(jnp.where(ok, green(cols, skeleton(skel_quad, other)), 0.0))
    far = split_dot(high[...], low[...], values[...]) * INV_FOUR_PI
    mine[0:128, :] = far[0:128]
    send[0:128, :] = far[128:256]


def final_kernel(near, near_got, low, low_got, move, basis, out):
    local_pair = low[128:256, :] + low_got[128:256, :]
    local = low[0:128, :] + low_got[0:128, :] + dot(move[0], local_pair)
    out[0] = near[...] + near_got[...] + three_dot(basis[0], local)


def near_scratch():
    return [
        pltpu.VMEM((512, 256), jnp.bfloat16),
        pltpu.VMEM((256, 128), jnp.float32),
    ]


def far_scratch(rows, n):
    wide = pltpu.VMEM((rows, 128 * n), jnp.bfloat16)
    return [wide, wide, pltpu.VMEM((128 * n, 256), jnp.bfloat16)]


NEAR_FLOPS = 2 * 6 * 512 * 512 * 128


def permute(value, target):
    n = lax.axis_size(AXIS)
    pairs = [(i, target(i)) for i in range(n)]
    return lax.ppermute(value, AXIS, [(i, j) for i, j in pairs if 0 <= j < n and i != j])


def swap(value, mask):
    return permute(value, lambda i: i ^ mask)


def listed_sum(own, entries, skels, coefs):
    def advance(running, partner):
        at = jnp.maximum(partner, 0)
        rows = skels[at]
        g = green([own[a][:, None] for a in range(3)], [rows[a][None, :] for a in range(3)]) * INV_FOUR_PI
        contrib = jnp.dot(g, coefs[at], precision=HIGHEST)
        return running + jnp.where(partner >= 0, contrib, 0.0), None

    return lax.scan(advance, jnp.zeros(coefs.shape[1:], jnp.float32), entries)[0]


def upper_anywhere(device, send, ctx, far_quad, far_top, skel_quad, skel_top):
    n = lax.axis_size(AXIS)
    part = lax.dynamic_slice_in_dim(send, device // 2 % 2 * 64, 64, 0)
    every = lax.all_gather(part, AXIS, axis=0, tiled=True).reshape(n // 4, 2, 2, 64, 128)
    quads = every[:, 0].reshape(n // 4, 128, 128)
    tops = every[:, 1].reshape(n // PLANE, 2, 128, 128).sum(axis=1)
    plane, quad = device // 8, device // 4
    local_top = listed_sum(skel_top[plane], far_top[plane], skel_top, tops)
    far = listed_sum(skel_quad[quad], far_quad[quad], skel_quad, quads)
    whole = jnp.concatenate([far, local_top], axis=0)
    return jnp.where(device % 2 == 0, whole, 0.0)


def per_device(
    vectors,
    points,
    leaf_basis,
    transfer_leaf,
    transfer_pair,
    transfer_quad,
    skel_leaf,
    skel_pair,
    skel_quad,
    skel_top,
    near_list,
    far_leaf,
    far_pair,
    far_quad,
    far_top,
):
    n = lax.axis_size(AXIS)
    device = lax.axis_index(AXIS)
    idx = device.reshape(1).astype(jnp.int32)
    def before(i):
        return i + 8 if i // 8 % 2 == 1 else i - 8

    ins = [vectors, leaf_basis, transfer_leaf]
    ins += [points.transpose(1, 0, 2), skel_leaf.transpose(1, 0, 2)]
    ins += [near_list, far_leaf]
    ship, keep, send = call(
        prepare_kernel,
        (f32(LEAF + PACK, 128), f32(64, 128), f32(80, 128)),
        [idx, *ins],
        n_smem=1,
        n_hbm=len(ins),
        scratch=[pltpu.VMEM(a.shape, a.dtype) for a in ins] + [pltpu.SemaphoreType.DMA((len(ins),))],
        flops=2 * 6 * 640 * 128 * 128,
        nbytes=1 << 20,
        vmem=60,
    )
    got = swap(send, 1)
    def near(slots, blocks, total, after):
        return call(
            functools.partial(near_kernel, slots),
            f32(1024, 128),
            [idx, got, own] + blocks + [total],
            n_smem=1,
            after=after,
            scratch=near_scratch(),
            flops=2 * len(slots) * NEAR_FLOPS,
        )

    bx, by, be = [swap(ship, m) for m in (2, 4, 8)]
    bo = permute(ship, before)
    rise, epair = call(rise_kernel, (f32(160, 128), f32(64, 128)), [keep, got, transfer_pair, transfer_quad], flops=2 * 6 * 64 * 128 * 128)
    rise_x = swap(rise, 2)
    total, own = call(
        own_kernel,
        (f32(1024, 128), f32(LEAF + PACK, 128)),
        [idx, got, ship],
        n_smem=1,
        n_hbm=1,
        after=[rise],
        scratch=near_scratch() + [pltpu.SemaphoreType.DMA],
        flops=2 * NEAR_FLOPS,
    )
    lists = [far_pair.T, far_quad, far_top] + [a.transpose(1, 0, 2) for a in (skel_pair, skel_quad, skel_top)]
    fetched = call(fetch_kernel, tuple(jax.ShapeDtypeStruct(a.shape, a.dtype) for a in lists), lists, after=[total])
    far_pair_t, far_quad_v, far_top_v, skel_pair_t, *skels = fetched
    half = call(quad_kernel, f32(256, 128), [rise, rise_x, epair], after=[fetched[0]])
    way = call(way_kernel, f32(LEAF + PACK, 128), [idx, bx, by], n_smem=1, after=[half])
    bd = permute(way, lambda i: i ^ 4 if i % 2 == 0 else i ^ 2)

    half_got = swap(half, 1)
    shared, ctx = call(
        top_kernel,
        (f32(128, 128), f32(256, 128)),
        [idx, half, half_got],
        n_smem=1,
        after=[way],
        scratch=[pltpu.VMEM((128, 128), jnp.float32), pltpu.VMEM((128, 128), jnp.float32)],
        flops=2 * 6 * 128**3,
    )
    direct = n == 4 * PLANE
    block = f32(LEAF + PACK, 128)
    total = near((1, 2), [bx, by], total, [shared])
    if direct:
        two = call(stack_kernel, f32(256, 128), [shared, swap(shared, PLANE)], after=[total])
    else:
        two = total
    sx, sy = call(cross_kernel, (block,) * 2, [idx, be, bo], n_smem=1, after=[two])
    cx, cy = swap(sx, 2), swap(sy, 4)
    cd = permute(bd, lambda i: i + 8 if i // 2 % 4 < 2 else i - 8)
    total = near((4, 5), [be, bo], total, [sx])
    if direct:
        quad_own, quad_send = call(
            upper_kernel,
            (f32(256, 128), f32(256, 128)),
            [idx, far_quad_v, far_top_v, two, swap(two, 2 * PLANE), *skels],
            n_smem=3,
            after=[total],
            scratch=far_scratch(256, 4) + [pltpu.VMEM((512, 128), jnp.float32)],
            flops=2 * 6 * 12 * 128**3,
        )
        quad_got = swap(quad_send, 4)
    else:
        quad_own = upper_anywhere(device, shared, ctx, far_quad, far_top, skel_quad, skel_top)
        quad_got = jnp.zeros_like(quad_own)
    total = near((3, 6, 7), [bd, cx, cy], total, [quad_own])
    mine, share = call(
        functools.partial(last_kernel, (8,)),
        (f32(512, 128), f32(512, 128)),
        [idx, got, own, cd, total],
        n_smem=1,
        scratch=[pltpu.VMEM((1024, 128), jnp.float32)] + near_scratch(),
        flops=2 * NEAR_FLOPS,
    )
    near_got = swap(share, 1)
    low, low_share = call(
        close_kernel,
        (f32(256, 128), f32(256, 128)),
        [idx, far_pair_t, got, own, skel_pair_t, ctx, quad_own, quad_got]
        + [bx, by, bd, be, bo, cx, cy, cd],
        n_smem=2,
        after=[share],
        scratch=[pltpu.VMEM((384, 128), jnp.float32)] + far_scratch(256, 9),
        flops=2 * 3 * 28 * 128**3,
    )
    return call(
        final_kernel,
        f32(1, 512, 128),
        [mine, near_got, low, swap(low_share, 1), transfer_leaf, leaf_basis],
        flops=2 * 6 * 640 * 128 * 128,
    )


def solution(mesh):
    placed = (
        P("leaf", None, None),
        P("leaf", None, None),
        P("leaf", None, None),
        P("leaf", None, None),
        P("leaf", None),
        P("leaf", None),
        P("leaf", None, None),
        P(),
        P(),
        P(),
        P("leaf", None),
        P("leaf", None),
        P(),
        P(),
        P(),
    )
    return jax.shard_map(
        per_device, mesh=mesh, in_specs=placed, out_specs=P("leaf", None, None), check_vma=False
    )
```

```python
import functools

import jax
import jax.numpy as jnp
from jax import lax
from jax.experimental import pallas as pl
from jax.experimental.pallas import tpu as pltpu
from jax.sharding import PartitionSpec as P

INV_FOUR_PI = 0.07957747154594767
DELTA_SQ = 0.01
HIGHEST = lax.Precision.HIGHEST
AXIS = "leaf"

PLANE = 8
NEAR_SLOTS = 16
FAR_SLOTS = 8

META = 0
COEF = 16
PART = 144
PACK = 272
LEAF = 512
STRIP = 16

VMEM = pl.BlockSpec(memory_space=pltpu.VMEM)
SMEM = pl.BlockSpec(memory_space=pltpu.SMEM)
HBM = pl.BlockSpec(memory_space=pl.ANY)


def call(body, outs, ins, n_smem=0, n_hbm=0, after=(), scratch=(), flops=0, nbytes=0, vmem=32):
    n, m = len(ins), len(after)

    def ordered(*refs):
        return body(*refs[:n], *refs[n + m :])

    return pl.pallas_call(
        ordered if after else body,
        out_shape=outs,
        in_specs=[SMEM] * n_smem + [VMEM] * (n - n_smem - n_hbm) + [HBM] * (n_hbm + m),
        out_specs=jax.tree.map(lambda _: VMEM, outs),
        scratch_shapes=list(scratch),
        compiler_params=pltpu.CompilerParams(vmem_limit_bytes=vmem * 1024 * 1024),
        cost_estimate=pl.CostEstimate(flops=flops, bytes_accessed=nbytes, transcendentals=0),
    )(*ins, *after)


def f32(*shape):
    return jax.ShapeDtypeStruct(shape, jnp.float32)


def dot(a, b):
    return jnp.dot(a, b, precision=HIGHEST, preferred_element_type=jnp.float32)


def dot_t(a, b):
    return lax.dot_general(
        a, b, (((0,), (0,)), ((), ())), precision=HIGHEST, preferred_element_type=jnp.float32
    )


def split(x):
    high = x.astype(jnp.bfloat16)
    return high, (x - high.astype(jnp.float32)).astype(jnp.bfloat16)


def put_values(values, span, x):
    values[span, 0:128], values[span, 128:256] = split(x)


def split_dot(high, low, values):
    both = jnp.dot(high, values, preferred_element_type=jnp.float32)
    rest = jnp.dot(low, values[:, 0:128], preferred_element_type=jnp.float32)
    return both[:, 0:128] + (both[:, 128:256] + rest)


def three_dot(a, b, contract=1):
    (ah, al), (bh, bl) = split(a), split(b)

    def one(x, y):
        return lax.dot_general(x, y, (((contract,), (0,)), ((), ())), preferred_element_type=jnp.float32)

    return one(ah, bh) + (one(ah, bl) + one(al, bh))


def columns(rows):
    pad = jnp.zeros((128 - rows.shape[0], 128), jnp.float32)
    return jnp.concatenate([rows, pad], axis=0).T


def green(cols, rows):
    dx = cols[0] - rows[0]
    dy = cols[1] - rows[1]
    dz = cols[2] - rows[2]
    return lax.rsqrt((dx * dx + dy * dy) + dz * dz + DELTA_SQ)


def skeleton(skel, cluster):
    return [skel[a, pl.ds(cluster, 1), :] for a in range(3)]


def own_columns(rows):
    cols = columns(jnp.concatenate(rows, axis=0))
    return [cols[:, a : a + 1] for a in range(3)]


def meta_skeleton(ref, at):
    return [ref[at + 4 * a + 3 : at + 4 * a + 4, :] for a in range(3)]


def window_bits(entry_at, count, base):
    bits = jnp.int32(0)
    for e in range(count):
        entry = entry_at(e)
        shift = jnp.clip(entry - base, 0, 31)
        bits = bits | jnp.where(entry >= 0, jnp.left_shift(jnp.int32(1), shift), 0)
    return bits


def leaf_bits(ref, at, start, count, leaf):
    row = ref[at + 15 : at + 16, :].astype(jnp.int32)
    lane = lax.broadcasted_iota(jnp.int32, (1, 128), 1)
    valid = (lane >= start) & (lane < start + count) & (row >= 0)
    shift = jnp.clip(row - (leaf - 9), 0, 23)
    one = jnp.where(valid, jnp.left_shift(jnp.ones_like(row), shift), 0)
    return jnp.sum(one.astype(jnp.float32)).astype(jnp.int32)


def has(bits, place):
    return (jnp.right_shift(bits, jnp.clip(place, 0, 31)) & 1) == 1


def chips_of(device):
    chip = device // 2
    place = chip % 4
    odd = (chip // 4) % 2
    out = [chip, chip ^ 1, chip ^ 2, chip ^ 3, chip ^ 4, chip + jnp.where(odd == 1, 4, -4)]
    for m in (1, 2, 3):
        other = place ^ m
        out.append((chip ^ m) + jnp.where(place < other, -4, 4))
    return out


def prepare_kernel(idx, *refs):
    names = 7
    ins, (ship, keep, send), bufs, sems = refs[:names], refs[names : names + 3], refs[names + 3 : -1], refs[-1]
    copies = [pltpu.make_async_copy(a, b, sems.at[k]) for k, (a, b) in enumerate(zip(ins, bufs))]
    for c in copies:
        c.start()
    for c in copies:
        c.wait()
    vec, basis, move, pts, skel, near_list, far_list = bufs
    core = idx[0] % 2
    pieces = []
    for k in range(4):
        for a in range(3):
            pieces.append(pts[a, :, 128 * k : 128 * (k + 1)])
        if k < 3:
            pieces.append(skel[k])
    rest = jnp.zeros((1, 128 - NEAR_SLOTS - FAR_SLOTS), jnp.float32)
    lists = [near_list[...].astype(jnp.float32), far_list[...].astype(jnp.float32), rest]
    pieces.append(jnp.concatenate(lists, axis=1))
    meta = jnp.concatenate(pieces, axis=0)
    coef = three_dot(basis[0], vec[0], 0)
    up = three_dot(move[0], coef, 0)
    ship[0:LEAF, :] = vec[0]
    ship[LEAF : LEAF + PACK, :] = jnp.concatenate([meta, coef, up], axis=0)
    low, high = up[:64], up[64:]
    keep[...] = jnp.where(core == 0, low, high)
    send[0:64, :] = jnp.where(core == 0, high, low)
    send[64:80, :] = meta


def add_near(device, slots, blocks, metas, total, scratch):
    values, cols = scratch
    core = device % 2
    chips = chips_of(device)
    bits = []
    for s, (ref, at) in enumerate(metas):
        bits.append(leaf_bits(ref, at, 0, NEAR_SLOTS, device ^ s))
        cols[128 * s : 128 * (s + 1), :] = columns(ref[at : at + 16, :])

    def with_sums(*sums):
        for slot, (vec, pack, at) in zip(slots, blocks):
            leaf = 2 * chips[slot] + core
            put_values(values, slice(0, LEAF), vec[0:LEAF, :] * INV_FOUR_PI)
            for s in range(2):
                listed = has(bits[s], leaf - ((device ^ s) - 9))
                for m in range(2):
                    half = values[256 * m : 256 * (m + 1), :]
                    pltpu.matmul_push_rhs(jnp.where(listed, half, jnp.zeros_like(half)), 0, m)
                for i in range(LEAF // STRIP):
                    start, piece = 128 * s + STRIP * i % 128, STRIP * i // 128
                    col = [
                        jnp.broadcast_to(cols[start : start + STRIP, 4 * piece + a : 4 * piece + a + 1], (STRIP, 128))
                        for a in range(3)
                    ]
                    for m in range(2):
                        parts = []
                        for k in (2 * m, 2 * m + 1):
                            row = [pack[at + 4 * k + a : at + 4 * k + a + 1, :] for a in range(3)]
                            parts.append(split(green(col, row)))
                        strip = sums[(s * (LEAF // STRIP) + i) * 2 + m]
                        for j in range(2):
                            side = jnp.concatenate([part[j] for part in parts], axis=1)
                            pltpu.matmul_acc_lhs(strip, side, 0 if i == 0 and j == 0 else None)
        for i in range(2 * LEAF // STRIP):
            both = pltpu.matmul_pop(sums[2 * i]) + pltpu.matmul_pop(sums[2 * i + 1])
            total[STRIP * i : STRIP * (i + 1), :] += both[:, 0:128] + both[:, 128:256]

    shape = (STRIP, 256)
    pl.run_scoped(with_sums, *[pltpu.ACC(m)(shape, jnp.float32) for _ in range(2 * LEAF // STRIP) for m in range(2)])


def add_far(device, slots, blocks, metas, far_pair, skel_pair, out, scratch):
    high, low, values = scratch
    n = len(slots)
    core = device % 2
    chips = chips_of(device)
    chip = device // 2
    n_chips = skel_pair.shape[1]
    depth = slice(0, 128 * n)
    bits = window_bits(lambda e: far_pair[e, chip], FAR_SLOTS, chip - 4)
    cols = own_columns(skeleton(skel_pair, chip))
    for j, (slot, (_, pack, at)) in enumerate(zip(slots, blocks)):
        other = chips[slot]
        span = slice(128 * j, 128 * (j + 1))
        put_values(values, span, pack[at + PART : at + PART + 128, :])
        g = green(cols, skeleton(skel_pair, jnp.clip(other, 0, n_chips - 1)))
        high[0:128, span], low[0:128, span] = split(jnp.where(has(bits, other - chip + 4), g, 0.0))
    out[256:384, :] += split_dot(high[0:128, depth], low[0:128, depth], values[depth, :]) * INV_FOUR_PI
    for j, (_, pack, at) in enumerate(blocks):
        put_values(values, slice(128 * j, 128 * (j + 1)), pack[at + COEF : at + COEF + 128, :])
    for s, (ref, base) in enumerate(metas):
        leaf = device ^ s
        bits = leaf_bits(ref, base, NEAR_SLOTS, FAR_SLOTS, leaf)
        cols = own_columns(meta_skeleton(ref, base))
        for j, (slot, (_, pack, at)) in enumerate(zip(slots, blocks)):
            g = green(cols, meta_skeleton(pack, at))
            ok = has(bits, 2 * chips[slot] + core - (leaf - 9))
            here = (slice(128 * s, 128 * (s + 1)), slice(128 * j, 128 * (j + 1)))
            high[here], low[here] = split(jnp.where(ok, g, 0.0))
    out[0:256, :] += split_dot(high[:, depth], low[:, depth], values[depth, :]) * INV_FOUR_PI


def own_kernel(idx, got, ship, total, own, *scratch):
    copy = pltpu.make_async_copy(ship, own, scratch[-1])
    copy.start()
    total[...] = jnp.zeros_like(total)
    copy.wait()
    add_near(idx[0], (0,), [(own, own, LEAF)], ((own, LEAF), (got, 64)), total, scratch[:-1])


def near_kernel(slots, idx, got, own, *refs):
    n = len(slots)
    blocks = [(b, b, LEAF) for b in refs[:n]]
    total_in, total, *scratch = refs[n:]
    total[...] = total_in[...]
    add_near(idx[0], slots, blocks, ((own, LEAF), (got, 64)), total, scratch)


def stack_kernel(*refs):
    out = refs[-1]
    for j, r in enumerate(refs[:-1]):
        out[128 * j : 128 * (j + 1), :] = r[...]


def cross_kernel(idx, even, odd, *outs):
    plane_odd = idx[0] // 8 % 2 == 1
    place = idx[0] // 2 % 4
    for m, out in zip((1, 2), outs):
        out[...] = jnp.where(((place ^ m) < place) == plane_odd, even[...], odd[...])


def fetch_kernel(*refs):
    half = len(refs) // 2
    for a, b in zip(refs[:half], refs[half:]):
        b[...] = a[...]


def way_kernel(idx, bx, by, out):
    out[...] = jnp.where(idx[0] % 2 == 0, bx[...], by[...])


def last_kernel(slots, idx, got, own, block, total_in, mine, share, total, *scratch):
    total[...] = total_in[...]
    add_near(idx[0], slots, [(block, block, LEAF)], ((own, LEAF), (got, 64)), total, scratch)
    mine[...] = total[0:512, :]
    share[...] = total[512:1024, :]


def far_kernel(idx, far_pair, got, own, skel_pair, *refs):
    blocks = [(b, b, LEAF) for b in (own,) + refs[:7]]
    low, *scratch = refs[7:]
    low[...] = jnp.zeros_like(low)
    add_far(idx[0], range(8), blocks, ((own, LEAF), (got, 64)), far_pair, skel_pair, low, scratch)


def close_kernel(idx, far_pair, got, own, skel_pair, ctx, quad_own, quad_got, low_in, cd, keep, share, low, *scratch):
    low[...] = low_in[...]
    add_far(idx[0], (8,), [(cd, cd, LEAF)], ((own, LEAF), (got, 64)), far_pair, skel_pair, low, scratch)
    local_top = quad_own[128:256, :] + quad_got[128:256, :]
    local_quad = quad_own[0:128, :] + quad_got[0:128, :] + dot(ctx[0:128, :], local_top)
    low[256:384, :] += dot(ctx[128:256, :], local_quad)
    keep[0:128, :] = low[0:128, :]
    keep[128:256, :] = low[256:384, :]
    share[...] = low[128:384, :]


def rise_kernel(keep, got, epair, equad, out, moved):
    moved[...] = epair[...]
    out[0:128, :] = dot_t(epair[...], keep[...] + got[0:64, :])
    out[128:160, :] = equad[...]


def quad_kernel(own, bx, epair, out):
    out[0:128, :] = own[0:128, :] + bx[0:128, :]
    out[128:160, :] = own[128:160, :]
    out[160:192, :] = bx[128:160, :]
    out[192:256, :] = epair[...]


def top_kernel(idx, mine, theirs, send, ctx, quad, top):
    device = idx[0]
    core = device % 2
    half = pl.multiple_of(core * 64, 64)
    for j in range(2):
        member = 2 * (((device // 2) ^ j) % 2)
        mine_at = pl.multiple_of((member + core) * 32, 32)
        sib_at = pl.multiple_of((member + 1 - core) * 32, 32)
        ctx[pl.ds(mine_at, 32), :] = mine[128 + 32 * j : 160 + 32 * j, :]
        ctx[pl.ds(sib_at, 32), :] = theirs[128 + 32 * j : 160 + 32 * j, :]
    ctx[pl.ds(128 + half, 64), :] = mine[192:256, :]
    ctx[pl.ds(192 - half, 64), :] = theirs[192:256, :]
    quad[...] = mine[0:128, :] + theirs[0:128, :]
    top[...] = dot_t(ctx[0:128, :], quad[...])
    send[0:64, :] = quad[pl.ds(half, 64), :]
    send[64:128, :] = top[pl.ds(half, 64), :]


def upper_kernel(idx, far_quad, far_top, two, others, skel_quad, skel_top, mine, send, high, low, values, rows):
    device = idx[0]
    half = pl.multiple_of((device % 2) * 64, 64)
    plane = device // 8
    quad = device // 4
    rows[...] = jnp.zeros_like(rows)
    for j in range(4):
        at = 128 * (j % 2)
        rows[pl.ds(128 * j + half, 64), :] = (two, others)[j // 2][at + 64 : at + 128, :]
    put_values(values, slice(0, 512), rows[...])
    bits = window_bits(lambda e: far_top[plane, e], FAR_SLOTS, 0)
    cols = own_columns(skeleton(skel_top, plane))
    for j in range(4):
        other = plane ^ j
        span = slice(128 * j, 128 * (j + 1))
        g = jnp.where(has(bits, other), green(cols, skeleton(skel_top, other)), 0.0)
        high[0:128, span], low[0:128, span] = split(g)
    top = split_dot(high[0:128, :], low[0:128, :], values[...]) * INV_FOUR_PI
    mine[128:256, :] = top
    send[128:256, :] = top
    for j in range(4):
        at = 128 * (j % 2)
        rows[pl.ds(128 * j + half, 64), :] = (two, others)[j // 2][at : at + 64, :]
    put_values(values, slice(0, 512), rows[...])
    for s in range(2):
        target = quad ^ s
        bits = window_bits(lambda e: far_quad[target, e], FAR_SLOTS, target - 4)
        cols = own_columns(skeleton(skel_quad, target))
        for j in range(4):
            other = quad ^ (2 * j)
            here = (slice(128 * s, 128 * (s + 1)), slice(128 * j, 128 * (j + 1)))
            ok = has(bits, other - target + 4) & (other >= target - 4) & (other <= target + 4)
            high[here], low[here] = split(jnp.where(ok, green(cols, skeleton(skel_quad, other)), 0.0))
    far = split_dot(high[...], low[...], values[...]) * INV_FOUR_PI
    mine[0:128, :] = far[0:128]
    send[0:128, :] = far[128:256]


def final_kernel(near, near_got, low, low_got, move, basis, out):
    local_pair = low[128:256, :] + low_got[128:256, :]
    local = low[0:128, :] + low_got[0:128, :] + dot(move[0], local_pair)
    out[0] = near[...] + near_got[...] + three_dot(basis[0], local)


def near_scratch():
    return [
        pltpu.VMEM((512, 256), jnp.bfloat16),
        pltpu.VMEM((256, 128), jnp.float32),
    ]


def far_scratch(rows, n):
    wide = pltpu.VMEM((rows, 128 * n), jnp.bfloat16)
    return [wide, wide, pltpu.VMEM((128 * n, 256), jnp.bfloat16)]


NEAR_FLOPS = 2 * 6 * 512 * 512 * 128


def permute(value, target):
    n = lax.axis_size(AXIS)
    pairs = [(i, target(i)) for i in range(n)]
    return lax.ppermute(value, AXIS, [(i, j) for i, j in pairs if 0 <= j < n and i != j])


def swap(value, mask):
    return permute(value, lambda i: i ^ mask)


def listed_sum(own, entries, skels, coefs):
    def advance(running, partner):
        at = jnp.maximum(partner, 0)
        rows = skels[at]
        g = green([own[a][:, None] for a in range(3)], [rows[a][None, :] for a in range(3)]) * INV_FOUR_PI
        contrib = jnp.dot(g, coefs[at], precision=HIGHEST)
        return running + jnp.where(partner >= 0, contrib, 0.0), None

    return lax.scan(advance, jnp.zeros(coefs.shape[1:], jnp.float32), entries)[0]


def upper_anywhere(device, send, ctx, far_quad, far_top, skel_quad, skel_top):
    n = lax.axis_size(AXIS)
    part = lax.dynamic_slice_in_dim(send, device // 2 % 2 * 64, 64, 0)
    every = lax.all_gather(part, AXIS, axis=0, tiled=True).reshape(n // 4, 2, 2, 64, 128)
    quads = every[:, 0].reshape(n // 4, 128, 128)
    tops = every[:, 1].reshape(n // PLANE, 2, 128, 128).sum(axis=1)
    plane, quad = device // 8, device // 4
    local_top = listed_sum(skel_top[plane], far_top[plane], skel_top, tops)
    far = listed_sum(skel_quad[quad], far_quad[quad], skel_quad, quads)
    whole = jnp.concatenate([far, local_top], axis=0)
    return jnp.where(device % 2 == 0, whole, 0.0)


def per_device(
    vectors,
    points,
    leaf_basis,
    transfer_leaf,
    transfer_pair,
    transfer_quad,
    skel_leaf,
    skel_pair,
    skel_quad,
    skel_top,
    near_list,
    far_leaf,
    far_pair,
    far_quad,
    far_top,
):
    n = lax.axis_size(AXIS)
    device = lax.axis_index(AXIS)
    idx = device.reshape(1).astype(jnp.int32)
    def before(i):
        return i + 8 if i // 8 % 2 == 1 else i - 8

    ins = [vectors, leaf_basis, transfer_leaf]
    ins += [points.transpose(1, 0, 2), skel_leaf.transpose(1, 0, 2)]
    ins += [near_list, far_leaf]
    ship, keep, send = call(
        prepare_kernel,
        (f32(LEAF + PACK, 128), f32(64, 128), f32(80, 128)),
        [idx, *ins],
        n_smem=1,
        n_hbm=len(ins),
        scratch=[pltpu.VMEM(a.shape, a.dtype) for a in ins] + [pltpu.SemaphoreType.DMA((len(ins),))],
        flops=2 * 6 * 640 * 128 * 128,
        nbytes=1 << 20,
        vmem=60,
    )
    got = swap(send, 1)
    def near(slots, blocks, total, after):
        return call(
            functools.partial(near_kernel, slots),
            f32(1024, 128),
            [idx, got, own] + blocks + [total],
            n_smem=1,
            after=after,
            scratch=near_scratch(),
            flops=2 * len(slots) * NEAR_FLOPS,
        )

    bx, by, be = [swap(ship, m) for m in (2, 4, 8)]
    bo = permute(ship, before)
    rise, epair = call(rise_kernel, (f32(160, 128), f32(64, 128)), [keep, got, transfer_pair, transfer_quad], flops=2 * 6 * 64 * 128 * 128)
    rise_x = swap(rise, 2)
    total, own = call(
        own_kernel,
        (f32(1024, 128), f32(LEAF + PACK, 128)),
        [idx, got, ship],
        n_smem=1,
        n_hbm=1,
        after=[rise],
        scratch=near_scratch() + [pltpu.SemaphoreType.DMA],
        flops=2 * NEAR_FLOPS,
    )
    lists = [far_pair.T, far_quad, far_top] + [a.transpose(1, 0, 2) for a in (skel_pair, skel_quad, skel_top)]
    fetched = call(fetch_kernel, tuple(jax.ShapeDtypeStruct(a.shape, a.dtype) for a in lists), lists, after=[total])
    far_pair_t, far_quad_v, far_top_v, skel_pair_t, *skels = fetched
    half = call(quad_kernel, f32(256, 128), [rise, rise_x, epair], after=[fetched[0]])
    way = call(way_kernel, f32(LEAF + PACK, 128), [idx, bx, by], n_smem=1, after=[half])
    bd = permute(way, lambda i: i ^ 4 if i % 2 == 0 else i ^ 2)

    half_got = swap(half, 1)
    shared, ctx = call(
        top_kernel,
        (f32(128, 128), f32(256, 128)),
        [idx, half, half_got],
        n_smem=1,
        after=[way],
        scratch=[pltpu.VMEM((128, 128), jnp.float32), pltpu.VMEM((128, 128), jnp.float32)],
        flops=2 * 6 * 128**3,
    )
    direct = n == 4 * PLANE
    block = f32(LEAF + PACK, 128)
    total = near((1, 2), [bx, by], total, [shared])
    if direct:
        two = call(stack_kernel, f32(256, 128), [shared, swap(shared, PLANE)], after=[total])
    else:
        two = total
    sx, sy = call(cross_kernel, (block,) * 2, [idx, be, bo], n_smem=1, after=[two])
    cx, cy = swap(sx, 2), swap(sy, 4)
    total = near((4, 5), [be, bo], total, [sx])
    bd_later = call(fetch_kernel, (block,), [bd], after=[total])[0]
    cd = permute(bd_later, lambda i: i + 8 if i // 2 % 4 < 2 else i - 8)
    if direct:
        quad_own, quad_send = call(
            upper_kernel,
            (f32(256, 128), f32(256, 128)),
            [idx, far_quad_v, far_top_v, two, swap(two, 2 * PLANE), *skels],
            n_smem=3,
            after=[total],
            scratch=far_scratch(256, 4) + [pltpu.VMEM((512, 128), jnp.float32)],
            flops=2 * 6 * 12 * 128**3,
        )
        quad_got = swap(quad_send, 4)
    else:
        quad_own = upper_anywhere(device, shared, ctx, far_quad, far_top, skel_quad, skel_top)
        quad_got = jnp.zeros_like(quad_own)
    total = near((3, 6, 7), [bd, cx, cy], total, [quad_own])
    far = call(
        far_kernel,
        f32(384, 128),
        [idx, far_pair_t, got, own, skel_pair_t, bx, by, bd, be, bo, cx, cy],
        n_smem=2,
        after=[total],
        scratch=far_scratch(256, 8),
        flops=2 * 3 * 25 * 128**3,
    )
    mine, share = call(
        functools.partial(last_kernel, (8,)),
        (f32(512, 128), f32(512, 128)),
        [idx, got, own, cd, total],
        n_smem=1,
        after=[far],
        scratch=[pltpu.VMEM((1024, 128), jnp.float32)] + near_scratch(),
        flops=2 * NEAR_FLOPS,
    )
    near_got = swap(share, 1)
    low, low_share = call(
        close_kernel,
        (f32(256, 128), f32(256, 128)),
        [idx, far_pair_t, got, own, skel_pair_t, ctx, quad_own, quad_got, far, cd],
        n_smem=2,
        after=[share],
        scratch=[pltpu.VMEM((384, 128), jnp.float32)] + far_scratch(256, 1),
        flops=2 * 3 * 28 * 128**3,
    )
    return call(
        final_kernel,
        f32(1, 512, 128),
        [mine, near_got, low, swap(low_share, 1), transfer_leaf, leaf_basis],
        flops=2 * 6 * 640 * 128 * 128,
    )


def solution(mesh):
    placed = (
        P("leaf", None, None),
        P("leaf", None, None),
        P("leaf", None, None),
        P("leaf", None, None),
        P("leaf", None),
        P("leaf", None),
        P("leaf", None, None),
        P(),
        P(),
        P(),
        P("leaf", None),
        P("leaf", None),
        P(),
        P(),
        P(),
    )
    return jax.shard_map(
        per_device, mesh=mesh, in_specs=placed, out_specs=P("leaf", None, None), check_vma=False
    )
```

```python
import functools

import jax
import jax.numpy as jnp
from jax import lax
from jax.experimental import pallas as pl
from jax.experimental.pallas import tpu as pltpu
from jax.sharding import PartitionSpec as P

INV_FOUR_PI = 0.07957747154594767
DELTA_SQ = 0.01
HIGHEST = lax.Precision.HIGHEST
AXIS = "leaf"

PLANE = 8
NEAR_SLOTS = 16
FAR_SLOTS = 8

META = 0
COEF = 16
PART = 144
PACK = 272
LEAF = 512
STRIP = 16

VMEM = pl.BlockSpec(memory_space=pltpu.VMEM)
SMEM = pl.BlockSpec(memory_space=pltpu.SMEM)
HBM = pl.BlockSpec(memory_space=pl.ANY)


def call(body, outs, ins, n_smem=0, n_hbm=0, after=(), scratch=(), flops=0, nbytes=0, vmem=32):
    n, m = len(ins), len(after)

    def ordered(*refs):
        return body(*refs[:n], *refs[n + m :])

    return pl.pallas_call(
        ordered if after else body,
        out_shape=outs,
        in_specs=[SMEM] * n_smem + [VMEM] * (n - n_smem - n_hbm) + [HBM] * (n_hbm + m),
        out_specs=jax.tree.map(lambda _: VMEM, outs),
        scratch_shapes=list(scratch),
        compiler_params=pltpu.CompilerParams(vmem_limit_bytes=vmem * 1024 * 1024),
        cost_estimate=pl.CostEstimate(flops=flops, bytes_accessed=nbytes, transcendentals=0),
    )(*ins, *after)


def f32(*shape):
    return jax.ShapeDtypeStruct(shape, jnp.float32)


def dot(a, b):
    return jnp.dot(a, b, precision=HIGHEST, preferred_element_type=jnp.float32)


def dot_t(a, b):
    return lax.dot_general(
        a, b, (((0,), (0,)), ((), ())), precision=HIGHEST, preferred_element_type=jnp.float32
    )


def split(x):
    high = x.astype(jnp.bfloat16)
    return high, (x - high.astype(jnp.float32)).astype(jnp.bfloat16)


def put_values(values, span, x):
    values[span, 0:128], values[span, 128:256] = split(x)


def split_dot(high, low, values):
    both = jnp.dot(high, values, preferred_element_type=jnp.float32)
    rest = jnp.dot(low, values[:, 0:128], preferred_element_type=jnp.float32)
    return both[:, 0:128] + (both[:, 128:256] + rest)


def three_dot(a, b, contract=1):
    (ah, al), (bh, bl) = split(a), split(b)

    def one(x, y):
        return lax.dot_general(x, y, (((contract,), (0,)), ((), ())), preferred_element_type=jnp.float32)

    return one(ah, bh) + (one(ah, bl) + one(al, bh))


def columns(rows):
    pad = jnp.zeros((128 - rows.shape[0], 128), jnp.float32)
    return jnp.concatenate([rows, pad], axis=0).T


def green(cols, rows):
    dx = cols[0] - rows[0]
    dy = cols[1] - rows[1]
    dz = cols[2] - rows[2]
    return lax.rsqrt((dx * dx + dy * dy) + dz * dz + DELTA_SQ)


def skeleton(skel, cluster):
    return [skel[a, pl.ds(cluster, 1), :] for a in range(3)]


def own_columns(rows):
    cols = columns(jnp.concatenate(rows, axis=0))
    return [cols[:, a : a + 1] for a in range(3)]


def meta_skeleton(ref, at):
    return [ref[at + 4 * a + 3 : at + 4 * a + 4, :] for a in range(3)]


def window_bits(entry_at, count, base):
    bits = jnp.int32(0)
    for e in range(count):
        entry = entry_at(e)
        shift = jnp.clip(entry - base, 0, 31)
        bits = bits | jnp.where(entry >= 0, jnp.left_shift(jnp.int32(1), shift), 0)
    return bits


def leaf_bits(ref, at, start, count, leaf):
    row = ref[at + 15 : at + 16, :].astype(jnp.int32)
    lane = lax.broadcasted_iota(jnp.int32, (1, 128), 1)
    valid = (lane >= start) & (lane < start + count) & (row >= 0)
    shift = jnp.clip(row - (leaf - 9), 0, 23)
    one = jnp.where(valid, jnp.left_shift(jnp.ones_like(row), shift), 0)
    return jnp.sum(one.astype(jnp.float32)).astype(jnp.int32)


def has(bits, place):
    return (jnp.right_shift(bits, jnp.clip(place, 0, 31)) & 1) == 1


def chips_of(device):
    chip = device // 2
    place = chip % 4
    odd = (chip // 4) % 2
    out = [chip, chip ^ 1, chip ^ 2, chip ^ 3, chip ^ 4, chip + jnp.where(odd == 1, 4, -4)]
    for m in (1, 2, 3):
        other = place ^ m
        out.append((chip ^ m) + jnp.where(place < other, -4, 4))
    return out


def prepare_kernel(idx, *refs):
    names = 7
    ins, (ship, keep, send), bufs, sems = refs[:names], refs[names : names + 3], refs[names + 3 : -1], refs[-1]
    copies = [pltpu.make_async_copy(a, b, sems.at[k]) for k, (a, b) in enumerate(zip(ins, bufs))]
    for c in copies:
        c.start()
    for c in copies:
        c.wait()
    vec, basis, move, pts, skel, near_list, far_list = bufs
    core = idx[0] % 2
    pieces = []
    for k in range(4):
        for a in range(3):
            pieces.append(pts[a, :, 128 * k : 128 * (k + 1)])
        if k < 3:
            pieces.append(skel[k])
    rest = jnp.zeros((1, 128 - NEAR_SLOTS - FAR_SLOTS), jnp.float32)
    lists = [near_list[...].astype(jnp.float32), far_list[...].astype(jnp.float32), rest]
    pieces.append(jnp.concatenate(lists, axis=1))
    meta = jnp.concatenate(pieces, axis=0)
    coef = three_dot(basis[0], vec[0], 0)
    up = three_dot(move[0], coef, 0)
    ship[0:LEAF, :] = vec[0]
    ship[LEAF : LEAF + PACK, :] = jnp.concatenate([meta, coef, up], axis=0)
    low, high = up[:64], up[64:]
    keep[...] = jnp.where(core == 0, low, high)
    send[0:64, :] = jnp.where(core == 0, high, low)
    send[64:80, :] = meta


def add_near(device, slots, blocks, metas, total, scratch):
    values, cols = scratch
    core = device % 2
    chips = chips_of(device)
    bits = []
    for s, (ref, at) in enumerate(metas):
        bits.append(leaf_bits(ref, at, 0, NEAR_SLOTS, device ^ s))
        cols[128 * s : 128 * (s + 1), :] = columns(ref[at : at + 16, :])

    def with_sums(*sums):
        for slot, (vec, pack, at) in zip(slots, blocks):
            leaf = 2 * chips[slot] + core
            put_values(values, slice(0, LEAF), vec[0:LEAF, :] * INV_FOUR_PI)
            for s in range(2):
                listed = has(bits[s], leaf - ((device ^ s) - 9))
                for m in range(2):
                    half = values[256 * m : 256 * (m + 1), :]
                    pltpu.matmul_push_rhs(jnp.where(listed, half, jnp.zeros_like(half)), 0, m)
                for i in range(LEAF // STRIP):
                    start, piece = 128 * s + STRIP * i % 128, STRIP * i // 128
                    col = [
                        jnp.broadcast_to(cols[start : start + STRIP, 4 * piece + a : 4 * piece + a + 1], (STRIP, 128))
                        for a in range(3)
                    ]
                    for m in range(2):
                        parts = []
                        for k in (2 * m, 2 * m + 1):
                            row = [pack[at + 4 * k + a : at + 4 * k + a + 1, :] for a in range(3)]
                            parts.append(split(green(col, row)))
                        strip = sums[(s * (LEAF // STRIP) + i) * 2 + m]
                        for j in range(2):
                            side = jnp.concatenate([part[j] for part in parts], axis=1)
                            pltpu.matmul_acc_lhs(strip, side, 0 if i == 0 and j == 0 else None)
        for i in range(2 * LEAF // STRIP):
            both = pltpu.matmul_pop(sums[2 * i]) + pltpu.matmul_pop(sums[2 * i + 1])
            total[STRIP * i : STRIP * (i + 1), :] += both[:, 0:128] + both[:, 128:256]

    shape = (STRIP, 256)
    pl.run_scoped(with_sums, *[pltpu.ACC(m)(shape, jnp.float32) for _ in range(2 * LEAF // STRIP) for m in range(2)])


def add_far(device, slots, blocks, metas, far_pair, skel_pair, out, scratch):
    high, low, values = scratch
    n = len(slots)
    core = device % 2
    chips = chips_of(device)
    chip = device // 2
    n_chips = skel_pair.shape[1]
    depth = slice(0, 128 * n)
    bits = window_bits(lambda e: far_pair[e, chip], FAR_SLOTS, chip - 4)
    cols = own_columns(skeleton(skel_pair, chip))
    for j, (slot, (_, pack, at)) in enumerate(zip(slots, blocks)):
        other = chips[slot]
        span = slice(128 * j, 128 * (j + 1))
        put_values(values, span, pack[at + PART : at + PART + 128, :])
        g = green(cols, skeleton(skel_pair, jnp.clip(other, 0, n_chips - 1)))
        high[0:128, span], low[0:128, span] = split(jnp.where(has(bits, other - chip + 4), g, 0.0))
    out[256:384, :] += split_dot(high[0:128, depth], low[0:128, depth], values[depth, :]) * INV_FOUR_PI
    for j, (_, pack, at) in enumerate(blocks):
        put_values(values, slice(128 * j, 128 * (j + 1)), pack[at + COEF : at + COEF + 128, :])
    for s, (ref, base) in enumerate(metas):
        leaf = device ^ s
        bits = leaf_bits(ref, base, NEAR_SLOTS, FAR_SLOTS, leaf)
        cols = own_columns(meta_skeleton(ref, base))
        for j, (slot, (_, pack, at)) in enumerate(zip(slots, blocks)):
            g = green(cols, meta_skeleton(pack, at))
            ok = has(bits, 2 * chips[slot] + core - (leaf - 9))
            here = (slice(128 * s, 128 * (s + 1)), slice(128 * j, 128 * (j + 1)))
            high[here], low[here] = split(jnp.where(ok, g, 0.0))
    out[0:256, :] += split_dot(high[:, depth], low[:, depth], values[depth, :]) * INV_FOUR_PI


def own_kernel(idx, got, ship, total, own, *scratch):
    copy = pltpu.make_async_copy(ship, own, scratch[-1])
    copy.start()
    total[...] = jnp.zeros_like(total)
    copy.wait()
    add_near(idx[0], (0,), [(own, own, LEAF)], ((own, LEAF), (got, 64)), total, scratch[:-1])


def near_kernel(slots, idx, got, own, *refs):
    n = len(slots)
    blocks = [(b, b, LEAF) for b in refs[:n]]
    total_in, total, *scratch = refs[n:]
    total[...] = total_in[...]
    add_near(idx[0], slots, blocks, ((own, LEAF), (got, 64)), total, scratch)


def stack_kernel(*refs):
    out = refs[-1]
    for j, r in enumerate(refs[:-1]):
        out[128 * j : 128 * (j + 1), :] = r[...]


def cross_kernel(idx, even, odd, *outs):
    plane_odd = idx[0] // 8 % 2 == 1
    place = idx[0] // 2 % 4
    for m, out in zip((1, 2), outs):
        out[...] = jnp.where(((place ^ m) < place) == plane_odd, even[...], odd[...])


def fetch_kernel(*refs):
    half = len(refs) // 2
    for a, b in zip(refs[:half], refs[half:]):
        b[...] = a[...]


def way_kernel(idx, bx, by, out):
    out[...] = jnp.where(idx[0] % 2 == 0, bx[...], by[...])


def last_kernel(slots, idx, got, own, block, total_in, mine, share, total, *scratch):
    total[...] = total_in[...]
    add_near(idx[0], slots, [(block, block, LEAF)], ((own, LEAF), (got, 64)), total, scratch)
    mine[...] = total[0:512, :]
    share[...] = total[512:1024, :]


def far_kernel(idx, far_pair, got, own, skel_pair, *refs):
    blocks = [(b, b, LEAF) for b in (own,) + refs[:7]]
    low, *scratch = refs[7:]
    low[...] = jnp.zeros_like(low)
    add_far(idx[0], range(8), blocks, ((own, LEAF), (got, 64)), far_pair, skel_pair, low, scratch)


def close_kernel(idx, far_pair, got, own, skel_pair, ctx, quad_own, quad_got, low_in, cd, keep, share, low, *scratch):
    low[...] = low_in[...]
    add_far(idx[0], (8,), [(cd, cd, LEAF)], ((own, LEAF), (got, 64)), far_pair, skel_pair, low, scratch)
    local_top = quad_own[128:256, :] + quad_got[128:256, :]
    local_quad = quad_own[0:128, :] + quad_got[0:128, :] + three_dot(ctx[0:128, :], local_top)
    low[256:384, :] += three_dot(ctx[128:256, :], local_quad)
    keep[0:128, :] = low[0:128, :]
    keep[128:256, :] = low[256:384, :]
    share[...] = low[128:384, :]


def rise_kernel(keep, got, epair, equad, out, moved):
    moved[...] = epair[...]
    out[0:128, :] = three_dot(epair[...], keep[...] + got[0:64, :], 0)
    out[128:160, :] = equad[...]


def quad_kernel(own, bx, epair, out):
    out[0:128, :] = own[0:128, :] + bx[0:128, :]
    out[128:160, :] = own[128:160, :]
    out[160:192, :] = bx[128:160, :]
    out[192:256, :] = epair[...]


def top_kernel(idx, mine, theirs, send, ctx, quad, top):
    device = idx[0]
    core = device % 2
    half = pl.multiple_of(core * 64, 64)
    for j in range(2):
        member = 2 * (((device // 2) ^ j) % 2)
        mine_at = pl.multiple_of((member + core) * 32, 32)
        sib_at = pl.multiple_of((member + 1 - core) * 32, 32)
        ctx[pl.ds(mine_at, 32), :] = mine[128 + 32 * j : 160 + 32 * j, :]
        ctx[pl.ds(sib_at, 32), :] = theirs[128 + 32 * j : 160 + 32 * j, :]
    ctx[pl.ds(128 + half, 64), :] = mine[192:256, :]
    ctx[pl.ds(192 - half, 64), :] = theirs[192:256, :]
    quad[...] = mine[0:128, :] + theirs[0:128, :]
    top[...] = three_dot(ctx[0:128, :], quad[...], 0)
    send[0:64, :] = quad[pl.ds(half, 64), :]
    send[64:128, :] = top[pl.ds(half, 64), :]


def upper_kernel(idx, far_quad, far_top, two, others, skel_quad, skel_top, mine, send, high, low, values, rows):
    device = idx[0]
    half = pl.multiple_of((device % 2) * 64, 64)
    plane = device // 8
    quad = device // 4
    rows[...] = jnp.zeros_like(rows)
    for j in range(4):
        at = 128 * (j % 2)
        rows[pl.ds(128 * j + half, 64), :] = (two, others)[j // 2][at + 64 : at + 128, :]
    put_values(values, slice(0, 512), rows[...])
    bits = window_bits(lambda e: far_top[plane, e], FAR_SLOTS, 0)
    cols = own_columns(skeleton(skel_top, plane))
    for j in range(4):
        other = plane ^ j
        span = slice(128 * j, 128 * (j + 1))
        g = jnp.where(has(bits, other), green(cols, skeleton(skel_top, other)), 0.0)
        high[0:128, span], low[0:128, span] = split(g)
    top = split_dot(high[0:128, :], low[0:128, :], values[...]) * INV_FOUR_PI
    mine[128:256, :] = top
    send[128:256, :] = top
    for j in range(4):
        at = 128 * (j % 2)
        rows[pl.ds(128 * j + half, 64), :] = (two, others)[j // 2][at : at + 64, :]
    put_values(values, slice(0, 512), rows[...])
    for s in range(2):
        target = quad ^ s
        bits = window_bits(lambda e: far_quad[target, e], FAR_SLOTS, target - 4)
        cols = own_columns(skeleton(skel_quad, target))
        for j in range(4):
            other = quad ^ (2 * j)
            here = (slice(128 * s, 128 * (s + 1)), slice(128 * j, 128 * (j + 1)))
            ok = has(bits, other - target + 4) & (other >= target - 4) & (other <= target + 4)
            high[here], low[here] = split(jnp.where(ok, green(cols, skeleton(skel_quad, other)), 0.0))
    far = split_dot(high[...], low[...], values[...]) * INV_FOUR_PI
    mine[0:128, :] = far[0:128]
    send[0:128, :] = far[128:256]


def final_kernel(near, near_got, low, low_got, move, basis, out):
    local_pair = low[128:256, :] + low_got[128:256, :]
    local = low[0:128, :] + low_got[0:128, :] + three_dot(move[0], local_pair)
    out[0] = near[...] + near_got[...] + three_dot(basis[0], local)


def near_scratch():
    return [
        pltpu.VMEM((512, 256), jnp.bfloat16),
        pltpu.VMEM((256, 128), jnp.float32),
    ]


def far_scratch(rows, n):
    wide = pltpu.VMEM((rows, 128 * n), jnp.bfloat16)
    return [wide, wide, pltpu.VMEM((128 * n, 256), jnp.bfloat16)]


NEAR_FLOPS = 2 * 6 * 512 * 512 * 128


def permute(value, target):
    n = lax.axis_size(AXIS)
    pairs = [(i, target(i)) for i in range(n)]
    return lax.ppermute(value, AXIS, [(i, j) for i, j in pairs if 0 <= j < n and i != j])


def swap(value, mask):
    return permute(value, lambda i: i ^ mask)


def listed_sum(own, entries, skels, coefs):
    def advance(running, partner):
        at = jnp.maximum(partner, 0)
        rows = skels[at]
        g = green([own[a][:, None] for a in range(3)], [rows[a][None, :] for a in range(3)]) * INV_FOUR_PI
        contrib = jnp.dot(g, coefs[at], precision=HIGHEST)
        return running + jnp.where(partner >= 0, contrib, 0.0), None

    return lax.scan(advance, jnp.zeros(coefs.shape[1:], jnp.float32), entries)[0]


def upper_anywhere(device, send, ctx, far_quad, far_top, skel_quad, skel_top):
    n = lax.axis_size(AXIS)
    part = lax.dynamic_slice_in_dim(send, device // 2 % 2 * 64, 64, 0)
    every = lax.all_gather(part, AXIS, axis=0, tiled=True).reshape(n // 4, 2, 2, 64, 128)
    quads = every[:, 0].reshape(n // 4, 128, 128)
    tops = every[:, 1].reshape(n // PLANE, 2, 128, 128).sum(axis=1)
    plane, quad = device // 8, device // 4
    local_top = listed_sum(skel_top[plane], far_top[plane], skel_top, tops)
    far = listed_sum(skel_quad[quad], far_quad[quad], skel_quad, quads)
    whole = jnp.concatenate([far, local_top], axis=0)
    return jnp.where(device % 2 == 0, whole, 0.0)


def per_device(
    vectors,
    points,
    leaf_basis,
    transfer_leaf,
    transfer_pair,
    transfer_quad,
    skel_leaf,
    skel_pair,
    skel_quad,
    skel_top,
    near_list,
    far_leaf,
    far_pair,
    far_quad,
    far_top,
):
    n = lax.axis_size(AXIS)
    device = lax.axis_index(AXIS)
    idx = device.reshape(1).astype(jnp.int32)
    def before(i):
        return i + 8 if i // 8 % 2 == 1 else i - 8

    ins = [vectors, leaf_basis, transfer_leaf]
    ins += [points.transpose(1, 0, 2), skel_leaf.transpose(1, 0, 2)]
    ins += [near_list, far_leaf]
    ship, keep, send = call(
        prepare_kernel,
        (f32(LEAF + PACK, 128), f32(64, 128), f32(80, 128)),
        [idx, *ins],
        n_smem=1,
        n_hbm=len(ins),
        scratch=[pltpu.VMEM(a.shape, a.dtype) for a in ins] + [pltpu.SemaphoreType.DMA((len(ins),))],
        flops=2 * 6 * 640 * 128 * 128,
        nbytes=1 << 20,
        vmem=60,
    )
    got = swap(send, 1)
    def near(slots, blocks, total, after):
        return call(
            functools.partial(near_kernel, slots),
            f32(1024, 128),
            [idx, got, own] + blocks + [total],
            n_smem=1,
            after=after,
            scratch=near_scratch(),
            flops=2 * len(slots) * NEAR_FLOPS,
        )

    bx, by, be = [swap(ship, m) for m in (2, 4, 8)]
    bo = permute(ship, before)
    rise, epair = call(rise_kernel, (f32(160, 128), f32(64, 128)), [keep, got, transfer_pair, transfer_quad], flops=2 * 6 * 64 * 128 * 128)
    rise_x = swap(rise, 2)
    total, own = call(
        own_kernel,
        (f32(1024, 128), f32(LEAF + PACK, 128)),
        [idx, got, ship],
        n_smem=1,
        n_hbm=1,
        after=[rise],
        scratch=near_scratch() + [pltpu.SemaphoreType.DMA],
        flops=2 * NEAR_FLOPS,
    )
    lists = [far_pair.T, far_quad, far_top] + [a.transpose(1, 0, 2) for a in (skel_pair, skel_quad, skel_top)]
    fetched = call(fetch_kernel, tuple(jax.ShapeDtypeStruct(a.shape, a.dtype) for a in lists), lists, after=[total])
    far_pair_t, far_quad_v, far_top_v, skel_pair_t, *skels = fetched
    half = call(quad_kernel, f32(256, 128), [rise, rise_x, epair], after=[fetched[0]])
    way = call(way_kernel, f32(LEAF + PACK, 128), [idx, bx, by], n_smem=1, after=[half])
    bd = permute(way, lambda i: i ^ 4 if i % 2 == 0 else i ^ 2)

    half_got = swap(half, 1)
    shared, ctx = call(
        top_kernel,
        (f32(128, 128), f32(256, 128)),
        [idx, half, half_got],
        n_smem=1,
        after=[way],
        scratch=[pltpu.VMEM((128, 128), jnp.float32), pltpu.VMEM((128, 128), jnp.float32)],
        flops=2 * 6 * 128**3,
    )
    direct = n == 4 * PLANE
    block = f32(LEAF + PACK, 128)
    total = near((1, 2), [bx, by], total, [shared])
    if direct:
        two = call(stack_kernel, f32(256, 128), [shared, swap(shared, PLANE)], after=[total])
    else:
        two = total
    sx, sy = call(cross_kernel, (block,) * 2, [idx, be, bo], n_smem=1, after=[two])
    cx, cy = swap(sx, 2), swap(sy, 4)
    total = near((4, 5), [be, bo], total, [sx])
    bd_later = call(fetch_kernel, (block,), [bd], after=[total])[0]
    cd = permute(bd_later, lambda i: i + 8 if i // 2 % 4 < 2 else i - 8)
    if direct:
        quad_own, quad_send = call(
            upper_kernel,
            (f32(256, 128), f32(256, 128)),
            [idx, far_quad_v, far_top_v, two, swap(two, 2 * PLANE), *skels],
            n_smem=3,
            after=[total],
            scratch=far_scratch(256, 4) + [pltpu.VMEM((512, 128), jnp.float32)],
            flops=2 * 6 * 12 * 128**3,
        )
        quad_got = swap(quad_send, 4)
    else:
        quad_own = upper_anywhere(device, shared, ctx, far_quad, far_top, skel_quad, skel_top)
        quad_got = jnp.zeros_like(quad_own)
    total = near((3, 6, 7), [bd, cx, cy], total, [quad_own])
    far = call(
        far_kernel,
        f32(384, 128),
        [idx, far_pair_t, got, own, skel_pair_t, bx, by, bd, be, bo, cx, cy],
        n_smem=2,
        after=[total],
        scratch=far_scratch(256, 8),
        flops=2 * 3 * 25 * 128**3,
    )
    mine, share = call(
        functools.partial(last_kernel, (8,)),
        (f32(512, 128), f32(512, 128)),
        [idx, got, own, cd, total],
        n_smem=1,
        after=[far],
        scratch=[pltpu.VMEM((1024, 128), jnp.float32)] + near_scratch(),
        flops=2 * NEAR_FLOPS,
    )
    near_got = swap(share, 1)
    low, low_share = call(
        close_kernel,
        (f32(256, 128), f32(256, 128)),
        [idx, far_pair_t, got, own, skel_pair_t, ctx, quad_own, quad_got, far, cd],
        n_smem=2,
        after=[share],
        scratch=[pltpu.VMEM((384, 128), jnp.float32)] + far_scratch(256, 1),
        flops=2 * 3 * 28 * 128**3,
    )
    return call(
        final_kernel,
        f32(1, 512, 128),
        [mine, near_got, low, swap(low_share, 1), transfer_leaf, leaf_basis],
        flops=2 * 6 * 640 * 128 * 128,
    )


def solution(mesh):
    placed = (
        P("leaf", None, None),
        P("leaf", None, None),
        P("leaf", None, None),
        P("leaf", None, None),
        P("leaf", None),
        P("leaf", None),
        P("leaf", None, None),
        P(),
        P(),
        P(),
        P("leaf", None),
        P("leaf", None),
        P(),
        P(),
        P(),
    )
    return jax.shard_map(
        per_device, mesh=mesh, in_specs=placed, out_specs=P("leaf", None, None), check_vma=False
    )
```
